512 devices in a mesh: blk: 128 (over x, z, y_hi, core), rep: 4 (over y_lo).
Axes of the slice: x: 4, y: 8 (y_hi: 2, y_lo: 4; y = y_hi * 4 + y_lo), z: 8, core: 2. Of those that a mesh axis runs over, the one named last changes fastest.
Arguments:
- texts: bfloat16 [2048, 512], P(('blk', 'rep')), may hold values from -5 to 5
- frames: bfloat16 [2048, 48, 512], P('blk'), may hold values from -30 to 30
- frame_mask: int32 [2048, 48], P('blk'), may hold values from 0 to 1, as said below
- cotangent: float32 [2048, 2048], P(None, 'blk'), may hold values from -24 to 24
Outputs:
- text_grad: bfloat16 [2048, 512], P(('blk', 'rep'))
- frame_grad: bfloat16 [2048, 48, 512], P(('blk', 'rep'))
The draws below stay inside these ranges and needn't reach their ends.
Inputs may be any that keep to these rules, and one draw needn't show every extreme that they name: `frame_mask`: each clip's real frames are its first n frames, 4 <= n <= 48; some clip has all 48.
All inputs are finite; a program needn't handle non-finite values.
Results may differ from the reference program's by a relative error of at most 0.015.
Values may be sent and summed in bfloat16 or wider, within the bound.
A program may use at most 64 MiB of HBM per device.

```python
import math
import jax
import jax.numpy as jnp
from jax import lax

D = 512
FR = 48
C_DEV = 16
CLIPS = 2048
TEXTS = 2048


def text_values(key):
    first_key = jax.random.fold_in(key, 0)
    gaussian = jnp.clip(jax.random.normal(first_key, (TEXTS, D), jnp.float32), -5.0, 5.0)
    return gaussian


def draw_texts(key, part):
    values = text_values(key)
    return values.astype(jnp.bfloat16)


def draw_frames(key, part):
    key = jax.random.fold_in(key, 7)
    first_key = jax.random.fold_in(key, 0)
    values = jnp.clip(jax.random.normal(first_key, (CLIPS, FR, D), jnp.float32), -5.0, 5.0)
    return values.astype(jnp.bfloat16)


def draw_frame_mask(key, part):
    key = jax.random.fold_in(key, 11)
    first_key, second_key = jax.random.split(key)
    groups = CLIPS // C_DEV
    level = jax.random.randint(first_key, (groups, 1), 0, 4)
    ceiling = 4 + (FR - 4) * (level + 1) // 4
    counts = jax.random.randint(second_key, (groups, C_DEV), 4, ceiling + 1).reshape(CLIPS)
    counts = counts.at[0].set(FR)
    return (jnp.arange(FR)[None, :] < counts[:, None]).astype(jnp.int32)


def raised(values, stream_key, source, target, parts, factor):
    def block_of(axis_at):
        return (jnp.arange(values.shape[axis_at]) // (values.shape[axis_at] // parts)).reshape((-1,) + (1,) * (values.ndim - 1 - axis_at))

    near = jax.random.permutation(stream_key, parts)[block_of(target)]
    other_side = (block_of(target) + parts // 2) % parts
    return jnp.where((block_of(source) == near) | (block_of(source) == other_side), factor * values, values)


def shard_levels(stream_key, extent, shards, least, top_value):
    def one(dim, shards_of):
        draws = jax.random.uniform(jax.random.fold_in(jax.random.fold_in(stream_key, 6), dim), (shards_of,), jnp.float32, least / len(shards), top_value / len(shards))
        return jnp.repeat(jnp.exp(draws), extent[dim] // shards_of).reshape((-1,) + (1,) * (len(extent) - dim - 1))

    gain = one(*shards[0])
    for cut in shards[1:]:
        gain = gain * one(*cut)
    return gain


def heavy_noise(stream_key, extent, width, bound, pieces, heavy, kind=jnp.bfloat16):
    entries = width * jax.random.normal(stream_key, extent, jnp.float32)
    if pieces:
        entries = entries * shard_levels(stream_key, extent, pieces, -0.22, 0.18)
    return jnp.clip(raised(entries, jax.random.fold_in(stream_key, 3), *heavy), -bound, bound).astype(kind)


def setup_inputs(seed: int = 0) -> dict:
    key_list = jax.random.split(jax.random.key(seed), 5)
    return {
        "texts": draw_texts(jax.random.fold_in(key_list[4], 71), 0),
        "frames": draw_frames(jax.random.fold_in(key_list[4], 71), 0),
        "frame_mask": draw_frame_mask(jax.random.fold_in(key_list[4], 71), 0),
        "cotangent": heavy_noise(key_list[3], (TEXTS, CLIPS), 1.0, 24.0, ((1, 128),), (1, 0, 128, 5.5), jnp.float32),
    }


EPSILON = 1e-05

def to_low(values):
    return lax.optimization_barrier(values.astype(jnp.bfloat16)).astype(jnp.float32)

def reference(texts, frames, frame_mask, cotangent):
    factor = 1.0 / math.sqrt(D)
    frames_wide = frames.astype(jnp.float32)
    live_mask = frame_mask > 0
    high = lax.Precision.HIGHEST
    block_rows = 8

    def step_block(frame_acc, inputs):
        text_rows, cot_rows = inputs
        text_wide = text_rows.astype(jnp.float32)
        scores = jnp.einsum('td,cfd->tcf', text_wide, frames_wide, precision=high) * factor
        scores = jnp.where(live_mask[None], scores, -1e+30)
        highest = lax.optimization_barrier(jnp.max(scores, axis=2, keepdims=True))
        raw_weights = jnp.exp(scores - highest)
        probs = raw_weights / lax.optimization_barrier(jnp.sum(raw_weights, axis=2, keepdims=True))
        probs_low = to_low(probs)
        pooled = jnp.einsum('tcf,cfd->tcd', probs_low, frames_wide, precision=high)
        inverse = lax.rsqrt(lax.optimization_barrier(jnp.mean(pooled * pooled, axis=2, keepdims=True)) + EPSILON)
        normed = pooled * inverse
        text_part = lax.optimization_barrier(jnp.sum(cot_rows[:, :, None] * normed, axis=1)) * factor
        upstream = cot_rows[:, :, None] * text_wide[:, None, :] * factor
        projected = lax.optimization_barrier(jnp.mean(upstream * normed, axis=2, keepdims=True))
        pooled_grad = inverse * (upstream - normed * projected)
        pooled_low = to_low(pooled_grad)
        prob_grad = jnp.einsum('tcd,cfd->tcf', pooled_low, frames_wide, precision=high)
        centred = lax.optimization_barrier(jnp.sum(probs * prob_grad, axis=2, keepdims=True))
        score_grad = probs * (prob_grad - centred)
        score_low = to_low(score_grad)
        frame_term = jnp.einsum('tcf,tcd->cfd', probs_low, pooled_low, precision=high)
        frame_term = frame_term + factor * jnp.einsum('tcf,td->cfd', score_low, text_wide, precision=high)
        text_term = text_part + factor * jnp.einsum('tcf,cfd->td', score_low, frames_wide, precision=high)
        return (frame_acc + frame_term, text_term)
    stacked = (texts.reshape(TEXTS // block_rows, block_rows, D), cotangent.reshape(TEXTS // block_rows, block_rows, CLIPS))
    zero_grads = jnp.zeros((CLIPS, FR, D), jnp.float32)
    frame_total, text_blocks = lax.scan(step_block, zero_grads, stacked)
    text_grad = text_blocks.reshape(TEXTS, D).astype(jnp.bfloat16)
    return (text_grad, frame_total.astype(jnp.bfloat16))
```

```python
import math

import jax
import jax.numpy as jnp
from jax import lax
from jax.experimental import pallas as pl
from jax.experimental.pallas import tpu as pltpu
from jax.sharding import PartitionSpec as P

MESH = pl.DeviceIdType.MESH
EPSILON = 1e-05
NX, NZ, NY = 4, 8, 8
D, FR, C_DEV, ROWS = 512, 48, 16, 4
CHUNK = 128
GROUP = 192
ORDER = (0, 1, 3, 2)
FACTOR = 1.0 / math.sqrt(D)
F32, BF16 = jnp.float32, jnp.bfloat16


def dot(a, b, ca, cb):
    return lax.dot_general(a, b, (((ca,), (cb,)), ((), ())), preferred_element_type=F32)


def swap(v):
    return pltpu.roll(v, 4, axis=1)


def tiles_to_rows(tiles):
    n = tiles.shape[0]
    pairs = tiles.reshape(n // 2, 2, 16, 128)
    low = lax.broadcasted_iota(jnp.int32, (n // 2, 8, 128), 1) < 4
    out = []
    for half in range(2):
        a = pairs[:, 0, 8 * half : 8 * half + 8]
        b = pairs[:, 1, 8 * half : 8 * half + 8]
        out.append(jnp.where(low, a, swap(b)).reshape(4 * n, 128))
        out.append(jnp.where(low, swap(a), b).reshape(4 * n, 128))
    return out


def rows_to_tiles(rows):
    n = rows.shape[0] // 4
    low = lax.broadcasted_iota(jnp.int32, (n // 2, 8, 128), 1) < 4
    blocks = [rows[:, 128 * k : 128 * k + 128].reshape(n // 2, 8, 128) for k in range(4)]
    first, second = [], []
    for half in range(2):
        a, b = blocks[2 * half], blocks[2 * half + 1]
        first.append(jnp.where(low, a, swap(b)))
        second.append(jnp.where(low, swap(a), b))
    first = jnp.concatenate(first, axis=1)
    second = jnp.concatenate(second, axis=1)
    return jnp.stack([first, second], axis=1).reshape(n, 16, 128)


def kernel(
    texts_ref, frames_ref, mask_ref, cot_ref, text_out, frame_out,
    frames, cot, z_texts, texts_in, texts, cot_sel, counts, gram_hi, gram_lo,
    probs_low, weights, scaled, text_tiles, core_send, core_recv, xy_send, xy_recv,
    z_send, z_recv, frame_send, frame_recv,
    load_sem, ag_z_send, ag_z_recv, ag_xy_send, ag_xy_recv, ag_c_send, ag_c_recv,
    rs_c_send, rs_c_recv, rs_xy_send, rs_xy_recv, rs_z_send, rs_z_recv, fr_send, fr_recv,
):
    blk, rep = lax.axis_index("blk"), lax.axis_index("rep")
    core = blk % 2
    y = (blk // 2) % 2 * 4 + rep
    z = blk // 4 % NZ
    x = blk // 32
    odd, half = y % 2, y // 2
    parity = half % 2
    handlers = ((2 * half + 1 - parity) % NY, (2 * half + NY - 1 + 3 * parity) % NY)
    pair = (half + parity + odd + 3) % 4
    slot = (half + 1 - odd) % 2
    own = slot == 0

    def device(xx, zz, yy, cc):
        return (((xx * NZ + zz) * 2 + yy // 4) * 2 + cc, yy % 4)

    sibling = device(x, z, y, 1 - core)

    def send(src, dst, send_sem, recv_sem, to):
        return pltpu.make_async_remote_copy(
            src_ref=src, dst_ref=dst, send_sem=send_sem, recv_sem=recv_sem, device_id=to, device_id_type=MESH
        )

    def arrived(ref, sem):
        pltpu.make_async_copy(ref, ref, sem).wait()

    loads = [pltpu.make_async_copy(cot_ref, cot, load_sem.at[4])]
    for g in range(4):
        loads.append(pltpu.make_async_copy(frames_ref.at[pl.ds(4 * g, 4)], frames.at[pl.ds(4 * g, 4)], load_sem.at[g]))
    for load in loads:
        load.start()

    barrier = pltpu.get_barrier_semaphore()

    def greet(to):
        pl.semaphore_signal(barrier, inc=1, device_id=to, device_id_type=MESH)

    greet(sibling)
    for dz in range(1, NZ):
        greet(device(x, (z + dz) % NZ, y, core))
    for k in range(1, 4):
        greet((blk, (rep + k) % 4))
    for dx in range(NX):
        xx = (x + dx) % NX
        for h in range(2):
            if dx == 0 and h == 0:

                @pl.when(jnp.logical_not(own))
                def _():
                    greet(device(x, z, handlers[0], core))
                    greet(device(x, z, 2 * pair + odd, core))

                greet(device(x, z, 2 * pair + 1 - odd, core))
            else:
                greet(device(xx, z, handlers[h], core))
                if dx > 0:
                    greet(device(xx, z, 2 * pair + h, core))

    rows = texts_ref[...].astype(F32)
    tile = jnp.concatenate([rows[:, 128 * k : 128 * k + 128] for k in range(4)], axis=0)
    z_texts[z] = tile.astype(BF16)

    @pl.when(own)
    def _():
        pl.semaphore_wait(barrier, 1 + 7 + 3 + 16 - 2)

    @pl.when(jnp.logical_not(own))
    def _():
        pl.semaphore_wait(barrier, 1 + 7 + 3 + 16)

    for dz in range(1, NZ):
        to = (z + dz) % NZ
        send(z_texts.at[z], z_texts.at[z], ag_z_send.at[dz], ag_z_recv.at[z], device(x, to, y, core)).start()

    pltpu.make_async_copy(cot_ref, cot, load_sem.at[4]).wait()
    picked = lax.broadcasted_iota(jnp.int32, (512, CHUNK), 0)
    lane = lax.broadcasted_iota(jnp.int32, (512, CHUNK), 1)
    wanted = (
        lane % 32 // 4 * 64 + pair // 2 * 32 + lane // 64 * 16 + pair % 2 * 8 + lane // 32 % 2 * 4 + lane % 4
    )
    choose = jnp.where(picked == wanted, 1.0, 0.0).astype(BF16)
    for xx in range(NX):
        wide = cot[:, 512 * xx : 512 * xx + 512]
        high = wide.astype(BF16)
        low = (wide - high.astype(F32)).astype(BF16)
        cot_sel[xx] = dot(high, choose, 1, 0) + dot(low, choose, 1, 0)
    totals = jnp.sum(mask_ref[...].astype(F32), axis=1, keepdims=True)
    counts[...] = jnp.broadcast_to(totals, (C_DEV, CHUNK))
    same = (
        lax.broadcasted_iota(jnp.int32, (GROUP, GROUP), 0) // FR
        == lax.broadcasted_iota(jnp.int32, (GROUP, GROUP), 1) // FR
    )

    def group_frames(g):
        return frames[4 * g : 4 * g + 4].reshape(GROUP, D)

    for g in range(4):
        loads[1 + g].wait()
        block = group_frames(g)
        gram = jnp.where(same, dot(block, block, 1, 1), 0.0)
        high = gram.astype(BF16)
        gram_hi[g] = high
        gram_lo[g] = (gram - high.astype(F32)).astype(BF16)

    for dz in range(1, NZ):
        source = (z + dz) % NZ
        arrived(z_texts.at[source], ag_z_recv.at[source])

    def to_handler(dx, h):
        xx = (x + dx) % NX
        return send(
            z_texts, texts_in.at[x, core, odd], ag_xy_send.at[dx, h], ag_xy_recv.at[x, odd],
            device(xx, z, handlers[h], core),
        )

    for dx in (2, 1, 3, 0):
        for h in range(2):
            if dx == 0 and h == 0:

                @pl.when(own)
                def _():
                    pltpu.make_async_copy(z_texts, texts_in.at[x, core, odd], ag_xy_recv.at[x, odd]).start()

                @pl.when(jnp.logical_not(own))
                def _():
                    to_handler(0, 0).start()
            else:
                to_handler(dx, h).start()

    def share(i):
        xx = (x + ORDER[i]) % NX
        for rr in range(2):
            arrived(texts_in.at[xx, core, rr], ag_xy_recv.at[xx, rr])
        send(texts_in.at[xx, core], texts_in.at[xx, core], ag_c_send.at[i], ag_c_recv.at[i], sibling).start()

    def work(i):
        xx = (x + ORDER[i]) % NX
        arrived(texts_in.at[xx, 1 - core], ag_c_recv.at[i])
        columns = slice(CHUNK * i, CHUNK * i + CHUNK)
        tiles = texts_in[xx].reshape(32, 16, 128).astype(F32)
        for k, block in enumerate(tiles_to_rows(tiles)):
            texts[columns, 128 * k : 128 * k + 128] = block.astype(BF16)
        chunk = texts[columns, :]
        cot_rows = cot_sel[xx]
        frame_index = lax.broadcasted_iota(jnp.int32, (FR, CHUNK), 0).astype(F32)
        for g in range(4):
            scores = dot(group_frames(g), chunk, 1, 1)
            kept = []
            for q in range(4):
                raw = scores[FR * q : FR * q + FR]
                live = frame_index < counts[4 * g + q : 4 * g + q + 1, :]
                masked = jnp.where(live, raw * FACTOR, -1e30)
                top = jnp.max(masked, axis=0, keepdims=True)
                grown = jnp.exp(masked - top)
                probs = grown * (1.0 / jnp.sum(grown, axis=0, keepdims=True))
                low = probs.astype(BF16)
                kept.append((raw, probs, low))
            group_low = jnp.concatenate([low for _, _, low in kept], axis=0)
            rows = slice(GROUP * g, GROUP * g + GROUP)
            probs_low[rows, columns] = group_low
            against = dot(gram_hi[g], group_low, 1, 0) + dot(gram_lo[g], group_low, 1, 0)
            for q in range(4):
                raw, probs, low = kept[q]
                low = low.astype(F32)
                with_pooled = against[FR * q : FR * q + FR]
                square = jnp.maximum(jnp.sum(low * with_pooled, axis=0, keepdims=True), 0.0)
                inner = jnp.sum(low * raw, axis=0, keepdims=True)
                inverse = lax.rsqrt(square * (1.0 / D) + EPSILON)
                up = inverse * cot_rows[4 * g + q : 4 * g + q + 1, :] * FACTOR
                back = up * inverse * inverse * inner * (1.0 / D)
                prob_grad = up * raw - back * with_pooled
                centred = jnp.sum(probs * prob_grad, axis=0, keepdims=True)
                score_grad = probs * (prob_grad - centred)
                at = slice(GROUP * g + FR * q, GROUP * g + FR * q + FR)
                weights[at, columns] = (up * low + FACTOR * score_grad).astype(BF16)
                scaled[at, columns] = (back * low).astype(BF16)
        part = dot(weights[:, columns], frames[...].reshape(C_DEV * FR, D), 0, 0)
        text_tiles[i] = rows_to_tiles(part).reshape(2, 16, 16, 128)
        core_send[i] = text_tiles[i, 1 - core].astype(BF16)
        send(core_send.at[i], core_recv.at[i], rs_c_send.at[i], rs_c_recv.at[i], sibling).start()

    def text_home(i, rr):
        xx = (x + ORDER[i]) % NX
        return send(
            xy_send.at[i, rr], xy_recv.at[x, slot], rs_xy_send.at[i, rr], rs_xy_recv.at[x, slot],
            device(xx, z, 2 * pair + rr, core),
        )

    def combine(i):
        arrived(core_recv.at[i], rs_c_recv.at[i])
        both = text_tiles[i, core] + core_recv[i].astype(F32)
        xy_send[i] = both.astype(BF16).reshape(2, NZ, 16, 128)
        for rr in range(2):
            if i == 0:
                stays = jnp.logical_and(own, odd == rr)

                @pl.when(stays)
                def _():
                    pltpu.make_async_copy(xy_send.at[0, rr], xy_recv.at[x, slot], rs_xy_recv.at[x, slot]).start()

                @pl.when(jnp.logical_not(stays))
                def _():
                    text_home(0, rr).start()
            else:
                text_home(i, rr).start()

    share(0)
    share(1)
    work(0)
    share(2)
    work(1)
    combine(0)
    share(3)
    work(2)
    combine(1)
    work(3)
    combine(2)

    def frame_home(g):
        return send(frame_send.at[g], frame_recv.at[rep], fr_send.at[g], fr_recv.at[rep], (blk, g))

    for g in range(4):
        rows = slice(GROUP * g, GROUP * g + GROUP)
        mixed = jnp.where(same, dot(scaled[rows, :], probs_low[rows, :], 1, 1), 0.0)
        grad = dot(weights[rows, :], texts[...], 1, 0) - dot(mixed.astype(BF16), group_frames(g), 1, 0)
        frame_send[g] = grad.astype(BF16)

        @pl.when(rep != g)
        def _():
            frame_home(g).start()

        if g == 0:
            combine(3)

    for h in range(2):
        for dx in ORDER:
            xx = (x + dx) % NX
            arrived(xy_recv.at[xx, h], rs_xy_recv.at[xx, h])
    z_send[...] = jnp.sum(xy_recv[...].reshape(8, NZ, 16, 128).astype(F32), axis=0).astype(BF16)
    for dz in range(1, NZ):
        to = (z + dz) % NZ
        send(z_send.at[to], z_recv.at[z], rs_z_send.at[dz], rs_z_recv.at[z], device(x, to, y, core)).start()
    z_recv[z] = z_send[z]

    total = frame_send[rep].astype(F32)
    for k in range(1, 4):
        source = (rep + k) % 4
        arrived(frame_recv.at[source], fr_recv.at[source])
        total = total + frame_recv[source].astype(F32)
    frame_out[...] = total.astype(BF16).reshape(4, FR, D)

    for dz in range(1, NZ):
        source = (z + dz) % NZ
        arrived(z_recv.at[source], rs_z_recv.at[source])
    tile = jnp.sum(z_recv[...].astype(F32), axis=0)
    text_out[...] = jnp.concatenate([tile[4 * k : 4 * k + 4] for k in range(4)], axis=1).astype(BF16)

    for dz in range(1, NZ):
        to = (z + dz) % NZ
        send(z_texts.at[z], z_texts.at[z], ag_z_send.at[dz], ag_z_recv.at[z], device(x, to, y, core)).wait_send()
        send(z_send.at[to], z_recv.at[z], rs_z_send.at[dz], rs_z_recv.at[z], device(x, to, y, core)).wait_send()
    for dx in range(NX):
        for h in range(2):
            if dx == 0 and h == 0:

                @pl.when(jnp.logical_not(own))
                def _():
                    to_handler(0, 0).wait_send()
            else:
                to_handler(dx, h).wait_send()
    for i in range(4):
        xx = (x + ORDER[i]) % NX
        send(texts_in.at[xx, core], texts_in.at[xx, core], ag_c_send.at[i], ag_c_recv.at[i], sibling).wait_send()
        send(core_send.at[i], core_recv.at[i], rs_c_send.at[i], rs_c_recv.at[i], sibling).wait_send()
        for rr in range(2):
            if i == 0:

                @pl.when(jnp.logical_not(jnp.logical_and(own, odd == rr)))
                def _():
                    text_home(0, rr).wait_send()
            else:
                text_home(i, rr).wait_send()
    for g in range(4):

        @pl.when(rep != g)
        def _():
            frame_home(g).wait_send()


def per_device(texts, frames, frame_mask, cotangent):
    vmem, dma = pltpu.VMEM, pltpu.SemaphoreType.DMA
    whole = pl.BlockSpec(memory_space=pltpu.VMEM)
    remote = pl.BlockSpec(memory_space=pl.ANY)
    clip_rows = C_DEV * FR
    return pl.pallas_call(
        kernel,
        out_shape=(
            jax.ShapeDtypeStruct((ROWS, D), BF16),
            jax.ShapeDtypeStruct((4, FR, D), BF16),
        ),
        in_specs=[whole, remote, whole, remote],
        out_specs=(whole, whole),
        scratch_shapes=[
            vmem((C_DEV, FR, D), BF16),
            vmem((C_DEV, 2048), F32),
            vmem((NZ, 16, 128), BF16),
            vmem((NX, 2, 2, NZ, 16, 128), BF16),
            vmem((4 * CHUNK, D), BF16),
            vmem((NX, C_DEV, CHUNK), F32),
            vmem((C_DEV, CHUNK), F32),
            vmem((4, GROUP, GROUP), BF16),
            vmem((4, GROUP, GROUP), BF16),
            vmem((clip_rows, 4 * CHUNK), BF16),
            vmem((clip_rows, 4 * CHUNK), BF16),
            vmem((clip_rows, 4 * CHUNK), BF16),
            vmem((4, 2, 16, 16, 128), F32),
            vmem((4, 16, 16, 128), BF16),
            vmem((4, 16, 16, 128), BF16),
            vmem((4, 2, NZ, 16, 128), BF16),
            vmem((NX, 2, NZ, 16, 128), BF16),
            vmem((NZ, 16, 128), BF16),
            vmem((NZ, 16, 128), BF16),
            vmem((4, GROUP, D), BF16),
            vmem((4, GROUP, D), BF16),
            dma((5,)), dma((NZ,)), dma((NZ,)), dma((NX, 2)), dma((NX, 2)), dma((4,)), dma((4,)),
            dma((4,)), dma((4,)), dma((4, 2)), dma((NX, 2)), dma((NZ,)), dma((NZ,)), dma((4,)), dma((4,)),
        ],
        compiler_params=pltpu.CompilerParams(
            collective_id=1, has_side_effects=True, vmem_limit_bytes=48 * 1024 * 1024
        ),
        name="pooling_grads",
    )(texts, frames, frame_mask, cotangent.T)


def solution(mesh):
    return jax.shard_map(
        per_device,
        mesh=mesh,
        in_specs=(P(("blk", "rep"), None), P("blk", None, None), P("blk", None), P(None, "blk")),
        out_specs=(P(("blk", "rep"), None), P(("blk", "rep"), None, None)),
        check_vma=False,
    )
```

```python
import math

import jax
import jax.numpy as jnp
from jax import lax
from jax.experimental import pallas as pl
from jax.experimental.pallas import tpu as pltpu
from jax.sharding import PartitionSpec as P

MESH = pl.DeviceIdType.MESH
EPSILON = 1e-05
NX, NZ, NY = 4, 8, 8
D, FR, C_DEV, ROWS = 512, 48, 16, 4
CHUNK = 128
GROUP = 192
VMEM_LIMIT = 48 * 1024 * 1024
FACTOR = 1.0 / math.sqrt(D)
F32, BF16 = jnp.float32, jnp.bfloat16


def dot(a, b, ca, cb):
    return lax.dot_general(a, b, (((ca,), (cb,)), ((), ())), preferred_element_type=F32)


def swap(v):
    return pltpu.roll(v, 4, axis=1)


def tiles_to_rows(tiles):
    n = tiles.shape[0]
    pairs = tiles.reshape(n // 2, 2, 16, 128)
    low = lax.broadcasted_iota(jnp.int32, (n // 2, 8, 128), 1) < 4
    out = []
    for half in range(2):
        a = pairs[:, 0, 8 * half : 8 * half + 8]
        b = pairs[:, 1, 8 * half : 8 * half + 8]
        out.append(jnp.where(low, a, swap(b)).reshape(4 * n, 128))
        out.append(jnp.where(low, swap(a), b).reshape(4 * n, 128))
    return out


def rows_to_tiles(rows):
    n = rows.shape[0] // 4
    low = lax.broadcasted_iota(jnp.int32, (n // 2, 8, 128), 1) < 4
    blocks = [rows[:, 128 * k : 128 * k + 128].reshape(n // 2, 8, 128) for k in range(4)]
    first, second = [], []
    for half in range(2):
        a, b = blocks[2 * half], blocks[2 * half + 1]
        first.append(jnp.where(low, a, swap(b)))
        second.append(jnp.where(low, swap(a), b))
    first = jnp.concatenate(first, axis=1)
    second = jnp.concatenate(second, axis=1)
    return jnp.stack([first, second], axis=1).reshape(n, 16, 128)


def kernel(
    texts_ref, frames_ref, mask_ref, cot_ref, text_out, frame_out,
    frames, cot, tile, texts_in, texts, cot_sel, counts, gram_hi, gram_lo,
    probs_low, weights, scaled, text_tiles, core_send, core_recv, home_send, home_recv,
    frame_send, frame_recv,
    load_sem, ag_xy_send, ag_xy_recv, ag_z_send, ag_z_recv, ag_c_send, ag_c_recv,
    rs_c_send, rs_c_recv, rs_send, rs_recv, fr_send, fr_recv,
):
    blk, rep = lax.axis_index("blk"), lax.axis_index("rep")
    core = blk % 2
    y = (blk // 2) % 2 * 4 + rep
    z = blk // 4 % NZ
    x = blk // 32
    odd, half = y % 2, y // 2
    parity = half % 2
    handlers = ((2 * half + 1 - parity) % NY, (2 * half + NY - 1 + 3 * parity) % NY)
    pair = (half + parity + odd + 3) % 4
    slot = (half + 1 - odd) % 2
    own = slot == 0

    def device(xx, zz, yy, cc):
        return (((xx * NZ + zz) * 2 + yy // 4) * 2 + cc, yy % 4)

    sibling = device(x, z, y, 1 - core)

    def send(src, dst, send_sem, recv_sem, to):
        return pltpu.make_async_remote_copy(
            src_ref=src, dst_ref=dst, send_sem=send_sem, recv_sem=recv_sem, device_id=to, device_id_type=MESH
        )

    started = []

    def start(copy, when=None):
        started.append((copy, when))
        if when is None:
            copy.start()
        else:
            pl.when(when)(copy.start)

    def drain():
        for copy, when in started:
            if when is None:
                copy.wait_send()
            else:
                pl.when(when)(copy.wait_send)

    def arrived(ref, sem):
        pltpu.make_async_copy(ref, ref, sem).wait()

    loads = [pltpu.make_async_copy(cot_ref, cot, load_sem.at[4])]
    for g in range(4):
        loads.append(pltpu.make_async_copy(frames_ref.at[pl.ds(4 * g, 4)], frames.at[pl.ds(4 * g, 4)], load_sem.at[g]))
    for load in loads:
        load.start()

    barrier = pltpu.get_barrier_semaphore()

    def greet(to):
        pl.semaphore_signal(barrier, inc=1, device_id=to, device_id_type=MESH)

    greet(sibling)
    for dz in (4, 3, 5, 2, 6, 1, 7):
        greet(device(x, (z + dz) % NZ, y, core))
    for dx in (2, 1, 3, 0):
        xx = (x + dx) % NX
        for h in range(2):
            if dx == 0 and h == 0:

                @pl.when(jnp.logical_not(own))
                def _():
                    greet(device(x, z, handlers[0], core))
                    greet(device(x, z, 2 * pair + odd, core))

                greet(device(x, z, 2 * pair + 1 - odd, core))
            else:
                greet(device(xx, z, handlers[h], core))
                if dx > 0:
                    greet(device(xx, z, 2 * pair + h, core))
    for k in range(1, 4):
        greet((blk, (rep + k) % 4))

    rows = texts_ref[...].astype(F32)
    tile[...] = jnp.concatenate([rows[:, 128 * k : 128 * k + 128] for k in range(4)], axis=0).astype(BF16)

    @pl.when(own)
    def _():
        pl.semaphore_wait(barrier, 1 + 7 + 3 + 16 - 2)

    @pl.when(jnp.logical_not(own))
    def _():
        pl.semaphore_wait(barrier, 1 + 7 + 3 + 16)

    mine = texts_in.at[z, core, 2 * x + odd]

    @pl.when(own)
    def _():
        pltpu.make_async_copy(tile, mine, ag_xy_recv).start()

    for dx in (2, 1, 3, 0):
        for h in range(2):
            to = device((x + dx) % NX, z, handlers[h], core)
            copy = send(tile, mine, ag_xy_send.at[dx, h], ag_xy_recv, to)
            start(copy, jnp.logical_not(own) if dx == 0 and h == 0 else None)

    loads[0].wait()
    picked = lax.broadcasted_iota(jnp.int32, (512, CHUNK), 0)
    lane = lax.broadcasted_iota(jnp.int32, (512, CHUNK), 1)
    wanted = (
        lane // 8 % 4 * 128 + lane // 64 * 64 + pair // 2 * 32 + lane // 32 % 2 * 16 + pair % 2 * 8 + lane % 8
    )
    choose = jnp.where(picked == wanted, 1.0, 0.0).astype(BF16)
    for k in range(4):
        wide = jnp.concatenate([cot[:, 512 * i + 128 * k : 512 * i + 128 * k + 128] for i in range(NX)], axis=1)
        high = wide.astype(BF16)
        low = (wide - high.astype(F32)).astype(BF16)
        cot_sel[k] = dot(high, choose, 1, 0) + dot(low, choose, 1, 0)
    totals = jnp.sum(mask_ref[...].astype(F32), axis=1, keepdims=True)
    counts[...] = jnp.broadcast_to(totals, (C_DEV, CHUNK))

    plane = texts_in.at[z, core]
    arrived(plane, ag_xy_recv)
    for dz in (4, 3, 5, 2, 6, 1, 7):
        start(send(plane, plane, ag_z_send.at[dz], ag_z_recv.at[z], device(x, (z + dz) % NZ, y, core)))

    same = (
        lax.broadcasted_iota(jnp.int32, (GROUP, GROUP), 0) // FR
        == lax.broadcasted_iota(jnp.int32, (GROUP, GROUP), 1) // FR
    )

    def group_frames(g):
        return frames[4 * g : 4 * g + 4].reshape(GROUP, D)

    for g in range(4):
        loads[1 + g].wait()
        block = group_frames(g)
        gram = jnp.where(same, dot(block, block, 1, 1), 0.0)
        high = gram.astype(BF16)
        gram_hi[g] = high
        gram_lo[g] = (gram - high.astype(F32)).astype(BF16)

    def share(k):
        for zz in (2 * k, 2 * k + 1):

            @pl.when(z != zz)
            def _():
                arrived(texts_in.at[zz, core], ag_z_recv.at[zz])

        both = texts_in.at[pl.ds(2 * k, 2), core]
        start(send(both, both, ag_c_send.at[k], ag_c_recv.at[k], sibling))

    def work(k):
        arrived(texts_in.at[pl.ds(2 * k, 2), 1 - core], ag_c_recv.at[k])
        columns = slice(CHUNK * k, CHUNK * k + CHUNK)
        tiles = texts_in[2 * k : 2 * k + 2].reshape(32, 16, 128).astype(F32)
        for i, block in enumerate(tiles_to_rows(tiles)):
            texts[columns, 128 * i : 128 * i + 128] = block.astype(BF16)
        chunk = texts[columns, :]
        cot_rows = cot_sel[k]
        frame_index = lax.broadcasted_iota(jnp.int32, (FR, CHUNK), 0).astype(F32)
        for g in range(4):
            scores = dot(group_frames(g), chunk, 1, 1)
            kept = []
            for q in range(4):
                raw = scores[FR * q : FR * q + FR]
                live = frame_index < counts[4 * g + q : 4 * g + q + 1, :]
                masked = jnp.where(live, raw * FACTOR, -1e30)
                top = jnp.max(masked, axis=0, keepdims=True)
                grown = jnp.exp(masked - top)
                probs = grown * (1.0 / jnp.sum(grown, axis=0, keepdims=True))
                low = probs.astype(BF16)
                kept.append((raw, probs, low))
            group_low = jnp.concatenate([low for _, _, low in kept], axis=0)
            rows = slice(GROUP * g, GROUP * g + GROUP)
            probs_low[rows, columns] = group_low
            against = dot(gram_hi[g], group_low, 1, 0) + dot(gram_lo[g], group_low, 1, 0)
            for q in range(4):
                raw, probs, low = kept[q]
                low = low.astype(F32)
                with_pooled = against[FR * q : FR * q + FR]
                square = jnp.maximum(jnp.sum(low * with_pooled, axis=0, keepdims=True), 0.0)
                inner = jnp.sum(low * raw, axis=0, keepdims=True)
                inverse = lax.rsqrt(square * (1.0 / D) + EPSILON)
                up = inverse * cot_rows[4 * g + q : 4 * g + q + 1, :] * FACTOR
                back = up * inverse * inverse * inner * (1.0 / D)
                prob_grad = up * raw - back * with_pooled
                centred = jnp.sum(probs * prob_grad, axis=0, keepdims=True)
                score_grad = probs * (prob_grad - centred)
                at = slice(GROUP * g + FR * q, GROUP * g + FR * q + FR)
                weights[at, columns] = (up * low + FACTOR * score_grad).astype(BF16)
                scaled[at, columns] = (back * low).astype(BF16)
        part = dot(weights[:, columns], frames[...].reshape(C_DEV * FR, D), 0, 0)
        text_tiles[k] = rows_to_tiles(part).reshape(2, 2, 8, 16, 128)
        core_send[k] = text_tiles[k, :, 1 - core].astype(BF16)
        start(send(core_send.at[k], core_recv.at[k], rs_c_send.at[k], rs_c_recv.at[k], sibling))

    def combine(k):
        arrived(core_recv.at[k], rs_c_recv.at[k])
        home_send[k] = (text_tiles[k, :, core] + core_recv[k].astype(F32)).astype(BF16)
        landing = home_recv.at[(x * NZ + z) * 2 + slot]
        for dx in (2, 1, 3, 0):
            xx = (x + dx) % NX
            for rr in range(2):
                for zz in range(2):
                    block = home_send.at[k, zz, 2 * xx + rr]
                    to = device(xx, 2 * k + zz, 2 * pair + rr, core)
                    copy = send(block, landing, rs_send.at[k, dx, rr, zz], rs_recv, to)
                    if dx == 0:
                        stays = jnp.logical_and(jnp.logical_and(own, odd == rr), z == 2 * k + zz)

                        @pl.when(stays)
                        def _():
                            pltpu.make_async_copy(block, landing, rs_recv).start()

                        start(copy, jnp.logical_not(stays))
                    else:
                        start(copy)

    share(0)
    share(1)
    work(0)
    share(2)
    work(1)
    combine(0)
    share(3)
    work(2)
    combine(1)
    work(3)
    combine(2)

    for g in range(4):
        rows = slice(GROUP * g, GROUP * g + GROUP)
        mixed = jnp.where(same, dot(scaled[rows, :], probs_low[rows, :], 1, 1), 0.0)
        grad = dot(weights[rows, :], texts[...], 1, 0) - dot(mixed.astype(BF16), group_frames(g), 1, 0)
        frame_send[g] = grad.astype(BF16)
        start(send(frame_send.at[g], frame_recv.at[rep], fr_send.at[g], fr_recv.at[rep], (blk, g)), rep != g)
        if g == 0:
            combine(3)

    total = frame_send[rep].astype(F32)
    for k in range(1, 4):
        source = (rep + k) % 4
        arrived(frame_recv.at[source], fr_recv.at[source])
        total = total + frame_recv[source].astype(F32)
    frame_out[...] = total.astype(BF16).reshape(4, FR, D)

    arrived(home_recv, rs_recv)
    summed = jnp.sum(home_recv[...].astype(F32), axis=0)
    text_out[...] = jnp.concatenate([summed[4 * k : 4 * k + 4] for k in range(4)], axis=1).astype(BF16)
    drain()


def per_device(texts, frames, frame_mask, cotangent):
    vmem, dma = pltpu.VMEM, pltpu.SemaphoreType.DMA
    whole = pl.BlockSpec(memory_space=pltpu.VMEM)
    remote = pl.BlockSpec(memory_space=pl.ANY)
    clip_rows = C_DEV * FR
    return pl.pallas_call(
        kernel,
        out_shape=(
            jax.ShapeDtypeStruct((ROWS, D), BF16),
            jax.ShapeDtypeStruct((4, FR, D), BF16),
        ),
        in_specs=[whole, remote, whole, remote],
        out_specs=(whole, whole),
        scratch_shapes=[
            vmem((C_DEV, FR, D), BF16),
            vmem((C_DEV, 2048), F32),
            vmem((16, 128), BF16),
            vmem((NZ, 2, 8, 16, 128), BF16),
            vmem((4 * CHUNK, D), BF16),
            vmem((4, C_DEV, CHUNK), F32),
            vmem((C_DEV, CHUNK), F32),
            vmem((4, GROUP, GROUP), BF16),
            vmem((4, GROUP, GROUP), BF16),
            vmem((clip_rows, 4 * CHUNK), BF16),
            vmem((clip_rows, 4 * CHUNK), BF16),
            vmem((clip_rows, 4 * CHUNK), BF16),
            vmem((4, 2, 2, 8, 16, 128), F32),
            vmem((4, 2, 8, 16, 128), BF16),
            vmem((4, 2, 8, 16, 128), BF16),
            vmem((4, 2, 8, 16, 128), BF16),
            vmem((64, 16, 128), BF16),
            vmem((4, GROUP, D), BF16),
            vmem((4, GROUP, D), BF16),
            dma((5,)), dma((NX, 2)), dma, dma((NZ,)), dma((NZ,)), dma((4,)), dma((4,)),
            dma((4,)), dma((4,)), dma((4, NX, 2, 2)), dma, dma((4,)), dma((4,)),
        ],
        compiler_params=pltpu.CompilerParams(
            collective_id=1, has_side_effects=True, vmem_limit_bytes=VMEM_LIMIT
        ),
        name="pooling_grads",
    )(*[pltpu.with_memory_space_constraint(v, pltpu.HBM) for v in (texts, frames, frame_mask, cotangent.T)])


def solution(mesh):
    return jax.shard_map(
        per_device,
        mesh=mesh,
        in_specs=(P(("blk", "rep"), None), P("blk", None, None), P("blk", None), P(None, "blk")),
        out_specs=(P(("blk", "rep"), None), P(("blk", "rep"), None, None)),
        check_vma=False,
    )
```

```python
import math

import jax
import jax.numpy as jnp
from jax import lax
from jax.experimental import pallas as pl
from jax.experimental.pallas import tpu as pltpu
from jax.sharding import PartitionSpec as P

MESH = pl.DeviceIdType.MESH
EPSILON = 1e-05
FAR_Z = (4, 3, 5, 2, 6, 1, 7, 0)
FAR_X = (2, 1, 3)
NX, NZ, NY = 4, 8, 8
D, FR, C_DEV, ROWS = 512, 48, 16, 4
CHUNK = 256
GROUP = 192
VMEM_LIMIT = 48 * 1024 * 1024
FACTOR = 1.0 / math.sqrt(D)
F32, BF16 = jnp.float32, jnp.bfloat16


def dot(a, b, ca, cb):
    return lax.dot_general(a, b, (((ca,), (cb,)), ((), ())), preferred_element_type=F32)


def swap(v):
    return pltpu.roll(v, 4, axis=1)


def tiles_to_rows(tiles):
    n = tiles.shape[0]
    pairs = tiles.reshape(n // 2, 2, 16, 128)
    low = lax.broadcasted_iota(jnp.int32, (n // 2, 8, 128), 1) < 4
    out = []
    for half in range(2):
        a = pairs[:, 0, 8 * half : 8 * half + 8]
        b = pairs[:, 1, 8 * half : 8 * half + 8]
        out.append(jnp.where(low, a, swap(b)).reshape(4 * n, 128))
        out.append(jnp.where(low, swap(a), b).reshape(4 * n, 128))
    return out


def rows_to_tiles(rows):
    n = rows.shape[0] // 4
    low = lax.broadcasted_iota(jnp.int32, (n // 2, 8, 128), 1) < 4
    blocks = [rows[:, 128 * k : 128 * k + 128].reshape(n // 2, 8, 128) for k in range(4)]
    first, second = [], []
    for half in range(2):
        a, b = blocks[2 * half], blocks[2 * half + 1]
        first.append(jnp.where(low, a, swap(b)))
        second.append(jnp.where(low, swap(a), b))
    first = jnp.concatenate(first, axis=1)
    second = jnp.concatenate(second, axis=1)
    return jnp.stack([first, second], axis=1).reshape(n, 16, 128)


def kernel(
    texts_ref, frames_ref, mask_ref, cot_ref, text_out, frame_out,
    frames, cot, tile, texts_in, texts, cot_sel, counts, gram_hi, gram_lo,
    probs_low, weights, scaled, text_tiles, core_send, core_recv, x_send, x_recv, home_send, home_recv,
    frame_send, frame_recv,
    load_sem, ag_send, ag_recv, ag_x_send, ag_x_recv, ag_c_send, ag_c_recv,
    rs_c_send, rs_c_recv, rs_x_send, rs_x_recv, rs_send, rs_recv, fr_send, fr_recv,
):
    blk, rep = lax.axis_index("blk"), lax.axis_index("rep")
    core = blk % 2
    high = blk // 2 % 2
    y = high * 4 + rep
    z = blk // 4 % NZ
    x = blk // 32
    inner = (rep + 1) // 2 % 2
    side = (high + 1 + inner) % 2
    clips = rep // 2 * 8
    place = rep % 2
    handlers = (4 * high + 1, 4 * high + 2, 4 - 4 * high, 7 - 4 * high)
    peers = tuple(4 * side + k for k in range(4)) + (4 - 4 * side + 1 - inner, 4 - 4 * side + 2 + inner)

    def device(xx, zz, yy, cc):
        return (((xx * NZ + zz) * 2 + yy // 4) * 2 + cc, yy % 4)

    sibling = device(x, z, y, 1 - core)
    partner = (blk, rep + 1 - 2 * place)

    def send(src, dst, send_sem, recv_sem, to):
        return pltpu.make_async_remote_copy(
            src_ref=src, dst_ref=dst, send_sem=send_sem, recv_sem=recv_sem, device_id=to, device_id_type=MESH
        )

    started = []

    def start(copy, when=None):
        started.append((copy, when))
        if when is None:
            copy.start()
        else:
            pl.when(when)(copy.start)

    def drain():
        for copy, when in started:
            if when is None:
                copy.wait_send()
            else:
                pl.when(when)(copy.wait_send)

    def arrived(ref, sem):
        pltpu.make_async_copy(ref, ref, sem).wait()

    loads = [pltpu.make_async_copy(cot_ref.at[pl.ds(clips, 8)], cot, load_sem.at[2])]
    for g in range(2):
        loads.append(
            pltpu.make_async_copy(
                frames_ref.at[pl.ds(clips + 4 * g, 4)], frames.at[pl.ds(4 * g, 4)], load_sem.at[g]
            )
        )
    for load in loads:
        load.start()

    barrier = pltpu.get_barrier_semaphore()

    def greet(to):
        pl.semaphore_signal(barrier, inc=1, device_id=to, device_id_type=MESH)

    for dz in FAR_Z:
        for k, yy in enumerate(peers):
            to = device(x, (z + dz) % NZ, yy, core)
            if dz == 0 and k < 4:
                pl.when(yy != y)(lambda to=to: greet(to))
            else:
                greet(to)
    for dx in FAR_X:
        greet(device((x + dx) % NX, z, y, core))
    greet(sibling)

    rows = texts_ref[...].astype(F32)
    tile[...] = jnp.concatenate([rows[:, 128 * k : 128 * k + 128] for k in range(4)], axis=0).astype(BF16)

    @pl.when(inner == 1)
    def _():
        pl.semaphore_wait(barrier, 8 * 6 + 3 + 1 - 1)

    @pl.when(inner == 0)
    def _():
        pl.semaphore_wait(barrier, 8 * 6 + 3 + 1)

    mine = texts_in.at[z, core, x, rep]
    for dz in FAR_Z:
        for k, yy in enumerate(handlers):
            copy = send(tile, mine, ag_send.at[dz, k], ag_recv.at[z], device(x, (z + dz) % NZ, yy, core))
            start(copy, yy != y if dz == 0 and k < 2 else None)

    @pl.when(inner == 1)
    def _():
        pltpu.make_async_copy(tile, mine, ag_recv.at[z]).start()

    loads[0].wait()
    picked = lax.broadcasted_iota(jnp.int32, (512, CHUNK), 0)
    lane = lax.broadcasted_iota(jnp.int32, (512, CHUNK), 1)
    wanted = lane // 16 % 4 * 128 + lane // 128 * 64 + side * 32 + lane // 64 % 2 * 16 + lane % 16
    choose = jnp.where(picked == wanted, 1.0, 0.0).astype(BF16)
    for k in range(4):
        wide = jnp.concatenate([cot[:, 512 * i + 128 * k : 512 * i + 128 * k + 128] for i in range(NX)], axis=1)
        upper = wide.astype(BF16)
        lower = (wide - upper.astype(F32)).astype(BF16)
        both = dot(jnp.concatenate([upper, lower], axis=0), choose, 1, 0)
        cot_sel[k] = both[:8] + both[8:]
    totals = jnp.sum(mask_ref[pl.ds(clips, 8), :].astype(F32), axis=1, keepdims=True)
    counts[...] = jnp.broadcast_to(totals, (8, CHUNK))
    same = (
        lax.broadcasted_iota(jnp.int32, (GROUP, GROUP), 0) // FR
        == lax.broadcasted_iota(jnp.int32, (GROUP, GROUP), 1) // FR
    )

    def group_frames(g):
        return frames[pl.ds(4 * g, 4)].reshape(GROUP, D)

    for g in range(2):
        loads[1 + g].wait()
        block = group_frames(g)
        gram = jnp.where(same, dot(block, block, 1, 1), 0.0)
        upper = gram.astype(BF16)
        gram_hi[g] = upper
        gram_lo[g] = (gram - upper.astype(F32)).astype(BF16)

    def spread(k):
        for zz in (2 * k, 2 * k + 1):
            arrived(texts_in.at[zz, core, x], ag_recv.at[zz])
        line = texts_in.at[pl.ds(2 * k, 2), core, x]
        for dx in FAR_X:
            start(send(line, line, ag_x_send.at[k, dx], ag_x_recv.at[k, x], device((x + dx) % NX, z, y, core)))

    def share(k):
        for dx in FAR_X:
            xx = (x + dx) % NX
            arrived(texts_in.at[pl.ds(2 * k, 2), core, xx], ag_x_recv.at[k, xx])
        both = texts_in.at[pl.ds(2 * k, 2), core]
        start(send(both, both, ag_c_send.at[k], ag_c_recv.at[k], sibling))

    def work(k):
        arrived(texts_in.at[pl.ds(2 * k, 2), 1 - core], ag_c_recv.at[k])
        columns = slice(CHUNK * k, CHUNK * k + CHUNK)
        tiles = texts_in[2 * k : 2 * k + 2].reshape(64, 16, 128).astype(F32)
        for i, block in enumerate(tiles_to_rows(tiles)):
            texts[columns, 128 * i : 128 * i + 128] = block.astype(BF16)
        chunk = texts[columns, :]
        cot_rows = cot_sel[k]
        frame_index = lax.broadcasted_iota(jnp.int32, (FR, CHUNK), 0).astype(F32)
        for g in range(2):
            scores = dot(group_frames(g), chunk, 1, 1)
            kept = []
            for q in range(4):
                raw = scores[FR * q : FR * q + FR]
                live = frame_index < counts[4 * g + q : 4 * g + q + 1, :]
                masked = jnp.where(live, raw * FACTOR, -1e30)
                top = jnp.max(masked, axis=0, keepdims=True)
                grown = jnp.exp(masked - top)
                probs = grown * (1.0 / jnp.sum(grown, axis=0, keepdims=True))
                low = probs.astype(BF16)
                kept.append((raw, probs, low))
            group_low = jnp.concatenate([low for _, _, low in kept], axis=0)
            probs_low[g, :, columns] = group_low
            against = dot(gram_hi[g], group_low, 1, 0) + dot(gram_lo[g], group_low, 1, 0)
            for q in range(4):
                raw, probs, low = kept[q]
                low = low.astype(F32)
                with_pooled = against[FR * q : FR * q + FR]
                square = jnp.maximum(jnp.sum(low * with_pooled, axis=0, keepdims=True), 0.0)
                inner_product = jnp.sum(low * raw, axis=0, keepdims=True)
                inverse = lax.rsqrt(square * (1.0 / D) + EPSILON)
                up = inverse * cot_rows[4 * g + q : 4 * g + q + 1, :] * FACTOR
                back = up * inverse * inverse * inner_product * (1.0 / D)
                prob_grad = up * raw - back * with_pooled
                centred = jnp.sum(probs * prob_grad, axis=0, keepdims=True)
                score_grad = probs * (prob_grad - centred)
                at = slice(FR * q, FR * q + FR)
                weights[g, at, columns] = (up * low + FACTOR * score_grad).astype(BF16)
                scaled[g, at, columns] = (back * low).astype(BF16)
        part = dot(weights[:, :, columns].reshape(8 * FR, CHUNK), frames[...].reshape(8 * FR, D), 0, 0)
        text_tiles[k] = rows_to_tiles(part).reshape(2, 2, NX, 4, 16, 128)
        core_send[k] = text_tiles[k, :, 1 - core].astype(BF16)
        start(send(core_send.at[k], core_recv.at[k], rs_c_send.at[k], rs_c_recv.at[k], sibling))

    def combine(k):
        arrived(core_recv.at[k], rs_c_recv.at[k])
        both = (text_tiles[k, :, core] + core_recv[k].astype(F32)).astype(BF16)
        for zz in range(2):
            x_send[k, :, zz] = both[zz]
        for dx in FAR_X:
            xx = (x + dx) % NX
            start(
                send(
                    x_send.at[k, xx], x_recv.at[k, dx - 1], rs_x_send.at[k, dx - 1], rs_x_recv.at[k, dx - 1],
                    device(xx, z, y, core),
                )
            )

    def deliver(k):
        total = x_send[k, x].astype(F32)
        for dx in FAR_X:
            arrived(x_recv.at[k, dx - 1], rs_x_recv.at[k, dx - 1])
            total = total + x_recv[k, dx - 1].astype(F32)
        home_send[k] = total.astype(BF16)
        landing = home_recv.at[z, rep]
        for zz in range(2):
            for m in range(4):
                block = home_send.at[k, zz, m]
                stays = jnp.logical_and(jnp.logical_and(inner == 1, rep == m), z == 2 * k + zz)
                copy = send(block, landing, rs_send.at[k, zz, m], rs_recv, device(x, 2 * k + zz, 4 * side + m, core))
                if m in (1, 2):

                    @pl.when(stays)
                    def _():
                        pltpu.make_async_copy(block, landing, rs_recv).start()

                    start(copy, jnp.logical_not(stays))
                else:
                    start(copy)

    def frame_grad(g):
        mixed = jnp.where(same, dot(scaled[g], probs_low[g], 1, 1), 0.0)
        return dot(weights[g], texts[...], 1, 0) - dot(mixed.astype(BF16), group_frames(g), 1, 0)

    for k in range(4):
        spread(k)
    share(0)
    share(1)
    work(0)
    share(2)
    work(1)
    combine(0)
    share(3)
    work(2)
    combine(1)
    work(3)
    combine(2)
    frame_send[...] = frame_grad(1 - place).astype(BF16)
    deliver(0)
    start(send(frame_send, frame_recv, fr_send, fr_recv, partner))
    combine(3)
    deliver(1)
    total = frame_grad(place)
    deliver(2)
    deliver(3)

    arrived(frame_recv, fr_recv)
    frame_out[...] = (total + frame_recv[...].astype(F32)).astype(BF16).reshape(4, FR, D)

    arrived(home_recv, rs_recv)
    summed = jnp.sum(home_recv[...].reshape(32, 16, 128).astype(F32), axis=0)
    text_out[...] = jnp.concatenate([summed[4 * k : 4 * k + 4] for k in range(4)], axis=1).astype(BF16)
    drain()


def per_device(texts, frames, frame_mask, cotangent):
    vmem, dma = pltpu.VMEM, pltpu.SemaphoreType.DMA
    whole = pl.BlockSpec(memory_space=pltpu.VMEM)
    remote = pl.BlockSpec(memory_space=pl.ANY)
    return pl.pallas_call(
        kernel,
        out_shape=(
            jax.ShapeDtypeStruct((ROWS, D), BF16),
            jax.ShapeDtypeStruct((4, FR, D), BF16),
        ),
        in_specs=[whole, remote, whole, remote],
        out_specs=(whole, whole),
        scratch_shapes=[
            vmem((8, FR, D), BF16),
            vmem((8, 2048), F32),
            vmem((16, 128), BF16),
            vmem((NZ, 2, NX, 4, 16, 128), BF16),
            vmem((4 * CHUNK, D), BF16),
            vmem((4, 8, CHUNK), F32),
            vmem((8, CHUNK), F32),
            vmem((2, GROUP, GROUP), BF16),
            vmem((2, GROUP, GROUP), BF16),
            vmem((2, GROUP, 4 * CHUNK), BF16),
            vmem((2, GROUP, 4 * CHUNK), BF16),
            vmem((2, GROUP, 4 * CHUNK), BF16),
            vmem((4, 2, 2, NX, 4, 16, 128), F32),
            vmem((4, 2, NX, 4, 16, 128), BF16),
            vmem((4, 2, NX, 4, 16, 128), BF16),
            vmem((4, NX, 2, 4, 16, 128), BF16),
            vmem((4, 3, 2, 4, 16, 128), BF16),
            vmem((4, 2, 4, 16, 128), BF16),
            vmem((NZ, 4, 16, 128), BF16),
            vmem((GROUP, D), BF16),
            vmem((GROUP, D), BF16),
            dma((3,)), dma((NZ, 4)), dma((NZ,)), dma((4, NX)), dma((4, NX)), dma((4,)), dma((4,)),
            dma((4,)), dma((4,)), dma((4, 3)), dma((4, 3)), dma((4, 2, 4)), dma, dma, dma,
        ],
        compiler_params=pltpu.CompilerParams(
            collective_id=1, has_side_effects=True, vmem_limit_bytes=VMEM_LIMIT
        ),
        name="pooling_grads",
    )(*[pltpu.with_memory_space_constraint(v, pltpu.HBM) for v in (texts, frames, frame_mask, cotangent.T)])


def solution(mesh):
    return jax.shard_map(
        per_device,
        mesh=mesh,
        in_specs=(P(("blk", "rep"), None), P("blk", None, None), P("blk", None), P(None, "blk")),
        out_specs=(P(("blk", "rep"), None), P(("blk", "rep"), None, None)),
        check_vma=False,
    )
```

```python
import math

import jax
import jax.numpy as jnp
from jax import lax
from jax.experimental import pallas as pl
from jax.experimental.pallas import tpu as pltpu
from jax.sharding import PartitionSpec as P

MESH = pl.DeviceIdType.MESH
EPSILON = 1e-05
FAR_Z = (4, 3, 5, 2, 6, 1, 7, 0)
FAR_X = (2, 1, 3)
NX, NZ, NY = 4, 8, 8
D, FR, C_DEV, ROWS = 512, 48, 16, 4
CHUNK = 128
GROUP = 192
VMEM_LIMIT = 48 * 1024 * 1024
FACTOR = 1.0 / math.sqrt(D)
F32, BF16 = jnp.float32, jnp.bfloat16


def dot(a, b, ca, cb):
    return lax.dot_general(a, b, (((ca,), (cb,)), ((), ())), preferred_element_type=F32)


def swap(v):
    return pltpu.roll(v, 4, axis=1)


def tiles_to_rows(tiles):
    n = tiles.shape[0]
    pairs = tiles.reshape(n // 2, 2, 16, 128)
    low = lax.broadcasted_iota(jnp.int32, (n // 2, 8, 128), 1) < 4
    out = []
    for half in range(2):
        a = pairs[:, 0, 8 * half : 8 * half + 8]
        b = pairs[:, 1, 8 * half : 8 * half + 8]
        out.append(jnp.where(low, a, swap(b)).reshape(4 * n, 128))
        out.append(jnp.where(low, swap(a), b).reshape(4 * n, 128))
    return out


def rows_to_tiles(rows):
    n = rows.shape[0] // 4
    low = lax.broadcasted_iota(jnp.int32, (n // 2, 8, 128), 1) < 4
    blocks = [rows[:, 128 * k : 128 * k + 128].reshape(n // 2, 8, 128) for k in range(4)]
    first, second = [], []
    for half in range(2):
        a, b = blocks[2 * half], blocks[2 * half + 1]
        first.append(jnp.where(low, a, swap(b)))
        second.append(jnp.where(low, swap(a), b))
    first = jnp.concatenate(first, axis=1)
    second = jnp.concatenate(second, axis=1)
    return jnp.stack([first, second], axis=1).reshape(n, 16, 128)


def kernel(
    texts_ref, frames_ref, mask_ref, cot_ref, text_out, frame_out,
    frames, cot, tile, texts_in, texts, cot_sel, counts, gram_hi, gram_lo,
    probs_low, weights, scaled, x_send, x_recv, home_send, home_recv,
    core_send, core_recv, frame_send, frame_recv,
    load_sem, swap_send, swap_recv, ag_send, ag_recv, ag_x_send, ag_x_recv,
    rs_x_send, rs_x_recv, rs_send, rs_recv, fr_c_send, fr_c_recv, fr_send, fr_recv,
):
    blk, rep = lax.axis_index("blk"), lax.axis_index("rep")
    core = blk % 2
    high = blk // 2 % 2
    y = high * 4 + rep
    z = blk // 4 % NZ
    x = blk // 32
    inner = (rep + 1) // 2 % 2
    side = (high + 1 + inner) % 2
    clips = rep // 2 * 8
    place = rep % 2
    handlers = (4 * high + 1, 4 * high + 2, 4 - 4 * high, 7 - 4 * high)
    peers = tuple(4 * side + k for k in range(4)) + (4 - 4 * side + 1 - inner, 4 - 4 * side + 2 + inner)

    def device(xx, zz, yy, cc):
        return (((xx * NZ + zz) * 2 + yy // 4) * 2 + cc, yy % 4)

    sibling = device(x, z, y, 1 - core)
    partner = (blk, rep + 1 - 2 * place)

    def send(src, dst, send_sem, recv_sem, to):
        return pltpu.make_async_remote_copy(
            src_ref=src, dst_ref=dst, send_sem=send_sem, recv_sem=recv_sem, device_id=to, device_id_type=MESH
        )

    started = []

    def start(copy, when=None):
        started.append((copy, when))
        if when is None:
            copy.start()
        else:
            pl.when(when)(copy.start)

    def drain():
        for copy, when in started:
            if when is None:
                copy.wait_send()
            else:
                pl.when(when)(copy.wait_send)

    def arrived(ref, sem):
        pltpu.make_async_copy(ref, ref, sem).wait()

    loads = [pltpu.make_async_copy(cot_ref.at[pl.ds(clips, 8)], cot.at[pl.ds(0, 8)], load_sem.at[2])]
    for g in range(2):
        loads.append(
            pltpu.make_async_copy(
                frames_ref.at[pl.ds(clips + 4 * g, 4)], frames.at[pl.ds(4 * g, 4)], load_sem.at[g]
            )
        )
    for load in loads:
        load.start()

    barrier = pltpu.get_barrier_semaphore()

    def greet(to):
        pl.semaphore_signal(barrier, inc=1, device_id=to, device_id_type=MESH)

    for dz in FAR_Z:
        for k, yy in enumerate(peers):
            to = device(x, (z + dz) % NZ, yy, core)
            if dz == 0 and k < 4:
                pl.when(yy != y)(lambda to=to: greet(to))
            else:
                greet(to)
    for dx in FAR_X:
        greet(device((x + dx) % NX, z, y, core))
    greet(sibling)

    totals = jnp.sum(mask_ref[pl.ds(clips, 8), :].astype(F32), axis=1, keepdims=True)
    counts[0] = jnp.broadcast_to(totals, (8, CHUNK))

    rows = texts_ref[...].astype(F32)
    tile[...] = jnp.concatenate([rows[:, 128 * k : 128 * k + 128] for k in range(4)], axis=0).astype(BF16)

    @pl.when(inner == 1)
    def _():
        pl.semaphore_wait(barrier, 8 * 6 + 3 + 1 - 1)

    @pl.when(inner == 0)
    def _():
        pl.semaphore_wait(barrier, 8 * 6 + 3 + 1)

    mine = texts_in.at[z, x, rep]
    for dz in FAR_Z:
        for k, yy in enumerate(handlers):
            copy = send(tile, mine, ag_send.at[dz, k], ag_recv.at[z], device(x, (z + dz) % NZ, yy, core))
            start(copy, yy != y if dz == 0 and k < 2 else None)

    @pl.when(inner == 1)
    def _():
        pltpu.make_async_copy(tile, mine, ag_recv.at[z]).start()

    for load in loads:
        load.wait()
    swaps = (
        (frames.at[pl.ds(0, 8)], frames.at[pl.ds(8, 8)]),
        (cot.at[pl.ds(0, 8)], cot.at[pl.ds(8, 8)]),
        (counts.at[0], counts.at[1]),
    )
    for k, (src, dst) in enumerate(swaps):
        start(send(src, dst, swap_send.at[k], swap_recv.at[k], sibling))

    picked = lax.broadcasted_iota(jnp.int32, (512, CHUNK), 0)
    lane = lax.broadcasted_iota(jnp.int32, (512, CHUNK), 1)
    wanted = lane // 16 % 4 * 128 + lane // 64 * 64 + side * 32 + core * 16 + lane % 16
    choose = jnp.where(picked == wanted, 1.0, 0.0).astype(BF16)
    for k, (src, dst) in enumerate(swaps):
        arrived(dst, swap_recv.at[k])
    for k in range(4):
        wide = jnp.concatenate([cot[:, 512 * i + 128 * k : 512 * i + 128 * k + 128] for i in range(NX)], axis=1)
        upper = wide.astype(BF16)
        lower = (wide - upper.astype(F32)).astype(BF16)
        both = dot(jnp.concatenate([upper, lower], axis=0), choose, 1, 0)
        cot_sel[k] = both[:16] + both[16:]
    same = (
        lax.broadcasted_iota(jnp.int32, (GROUP, GROUP), 0) // FR
        == lax.broadcasted_iota(jnp.int32, (GROUP, GROUP), 1) // FR
    )

    def group_frames(g):
        return frames[pl.ds(4 * g, 4)].reshape(GROUP, D)

    for g in range(4):
        block = group_frames(g)
        gram = jnp.where(same, dot(block, block, 1, 1), 0.0)
        upper = gram.astype(BF16)
        gram_hi[g] = upper
        gram_lo[g] = (gram - upper.astype(F32)).astype(BF16)

    def spread(k):
        for zz in (2 * k, 2 * k + 1):
            arrived(texts_in.at[zz, x], ag_recv.at[zz])
        line = texts_in.at[pl.ds(2 * k, 2), x]
        for dx in FAR_X:
            start(send(line, line, ag_x_send.at[k, dx], ag_x_recv.at[k, x], device((x + dx) % NX, z, y, core)))

    def work(k):
        for dx in FAR_X:
            xx = (x + dx) % NX
            arrived(texts_in.at[pl.ds(2 * k, 2), xx], ag_x_recv.at[k, xx])
        columns = slice(CHUNK * k, CHUNK * k + CHUNK)
        tiles = texts_in[2 * k : 2 * k + 2].reshape(32, 16, 128).astype(F32)
        for i, block in enumerate(tiles_to_rows(tiles)):
            texts[columns, 128 * i : 128 * i + 128] = block.astype(BF16)
        chunk = texts[columns, :]
        frame_index = lax.broadcasted_iota(jnp.int32, (FR, CHUNK), 0).astype(F32)
        for g in range(4):
            scores = dot(group_frames(g), chunk, 1, 1)
            kept = []
            for q in range(4):
                c = 4 * g + q
                raw = scores[FR * q : FR * q + FR]
                live = frame_index < counts[c // 8, c % 8 : c % 8 + 1, :]
                masked = jnp.where(live, raw * FACTOR, -1e30)
                top = jnp.max(masked, axis=0, keepdims=True)
                grown = jnp.exp(masked - top)
                probs = grown * (1.0 / jnp.sum(grown, axis=0, keepdims=True))
                low = probs.astype(BF16)
                kept.append((raw, probs, low))
            group_low = jnp.concatenate([low for _, _, low in kept], axis=0)
            probs_low[g, :, columns] = group_low
            against = dot(gram_hi[g], group_low, 1, 0) + dot(gram_lo[g], group_low, 1, 0)
            for q in range(4):
                c = 4 * g + q
                raw, probs, low = kept[q]
                low = low.astype(F32)
                with_pooled = against[FR * q : FR * q + FR]
                square = jnp.maximum(jnp.sum(low * with_pooled, axis=0, keepdims=True), 0.0)
                inner_product = jnp.sum(low * raw, axis=0, keepdims=True)
                inverse = lax.rsqrt(square * (1.0 / D) + EPSILON)
                up = inverse * cot_sel[k, c : c + 1, :] * FACTOR
                back = up * inverse * inverse * inner_product * (1.0 / D)
                prob_grad = up * raw - back * with_pooled
                centred = jnp.sum(probs * prob_grad, axis=0, keepdims=True)
                score_grad = probs * (prob_grad - centred)
                at = slice(FR * q, FR * q + FR)
                weights[g, at, columns] = (up * low + FACTOR * score_grad).astype(BF16)
                scaled[g, at, columns] = (back * low).astype(BF16)
        part = dot(weights[:, :, columns].reshape(16 * FR, CHUNK), frames[...].reshape(16 * FR, D), 0, 0)
        blocks = rows_to_tiles(part).astype(BF16).reshape(2, NX, 4, 16, 128)
        for zz in range(2):
            x_send[k, :, zz] = blocks[zz]
        for dx in FAR_X:
            xx = (x + dx) % NX
            start(
                send(
                    x_send.at[k, xx], x_recv.at[k, dx - 1], rs_x_send.at[k, dx - 1], rs_x_recv.at[k, dx - 1],
                    device(xx, z, y, core),
                )
            )

    def deliver(k):
        total = x_send[k, x].astype(F32)
        for dx in FAR_X:
            arrived(x_recv.at[k, dx - 1], rs_x_recv.at[k, dx - 1])
            total = total + x_recv[k, dx - 1].astype(F32)
        home_send[k] = total.astype(BF16)
        landing = home_recv.at[z, rep]
        for zz in range(2):
            for m in range(4):
                block = home_send.at[k, zz, m]
                stays = jnp.logical_and(jnp.logical_and(inner == 1, rep == m), z == 2 * k + zz)
                copy = send(block, landing, rs_send.at[k, zz, m], rs_recv, device(x, 2 * k + zz, 4 * side + m, core))
                if m in (1, 2):

                    @pl.when(stays)
                    def _():
                        pltpu.make_async_copy(block, landing, rs_recv).start()

                    start(copy, jnp.logical_not(stays))
                else:
                    start(copy)

    def frame_grad(g):
        mixed = jnp.where(same, dot(scaled[g], probs_low[g], 1, 1), 0.0)
        return dot(weights[g], texts[...], 1, 0) - dot(mixed.astype(BF16), group_frames(g), 1, 0)

    def to_sibling(k, g):
        core_send[k] = frame_grad(2 + g).astype(BF16)
        start(send(core_send.at[k], core_recv.at[k], fr_c_send.at[k], fr_c_recv.at[k], sibling))

    def from_sibling(k, g):
        grad = frame_grad(g)
        arrived(core_recv.at[k], fr_c_recv.at[k])
        return grad + core_recv[k].astype(F32)

    for k in range(4):
        spread(k)
    work(0)
    work(1)
    work(2)
    work(3)
    to_sibling(0, 1 - place)
    deliver(0)
    deliver(1)
    frame_send[...] = from_sibling(0, 1 - place).astype(BF16)
    deliver(2)
    start(send(frame_send, frame_recv, fr_send, fr_recv, partner))
    to_sibling(1, place)
    total = from_sibling(1, place)
    deliver(3)

    arrived(frame_recv, fr_recv)
    frame_out[...] = (total + frame_recv[...].astype(F32)).astype(BF16).reshape(4, FR, D)

    arrived(home_recv, rs_recv)
    summed = jnp.sum(home_recv[...].reshape(32, 16, 128).astype(F32), axis=0)
    text_out[...] = jnp.concatenate([summed[4 * k : 4 * k + 4] for k in range(4)], axis=1).astype(BF16)
    drain()


def per_device(texts, frames, frame_mask, cotangent):
    vmem, dma = pltpu.VMEM, pltpu.SemaphoreType.DMA
    whole = pl.BlockSpec(memory_space=pltpu.VMEM)
    remote = pl.BlockSpec(memory_space=pl.ANY)
    return pl.pallas_call(
        kernel,
        out_shape=(
            jax.ShapeDtypeStruct((ROWS, D), BF16),
            jax.ShapeDtypeStruct((4, FR, D), BF16),
        ),
        in_specs=[whole, remote, whole, remote],
        out_specs=(whole, whole),
        scratch_shapes=[
            vmem((16, FR, D), BF16),
            vmem((16, 2048), F32),
            vmem((16, 128), BF16),
            vmem((NZ, NX, 4, 16, 128), BF16),
            vmem((4 * CHUNK, D), BF16),
            vmem((4, 16, CHUNK), F32),
            vmem((2, 8, CHUNK), F32),
            vmem((4, GROUP, GROUP), BF16),
            vmem((4, GROUP, GROUP), BF16),
            vmem((4, GROUP, 4 * CHUNK), BF16),
            vmem((4, GROUP, 4 * CHUNK), BF16),
            vmem((4, GROUP, 4 * CHUNK), BF16),
            vmem((4, NX, 2, 4, 16, 128), BF16),
            vmem((4, 3, 2, 4, 16, 128), BF16),
            vmem((4, 2, 4, 16, 128), BF16),
            vmem((NZ, 4, 16, 128), BF16),
            vmem((2, GROUP, D), BF16),
            vmem((2, GROUP, D), BF16),
            vmem((GROUP, D), BF16),
            vmem((GROUP, D), BF16),
            dma((3,)), dma((3,)), dma((3,)), dma((NZ, 4)), dma((NZ,)), dma((4, NX)), dma((4, NX)),
            dma((4, 3)), dma((4, 3)), dma((4, 2, 4)), dma, dma((2,)), dma((2,)), dma, dma,
        ],
        compiler_params=pltpu.CompilerParams(
            collective_id=1, has_side_effects=True, vmem_limit_bytes=VMEM_LIMIT
        ),
        name="pooling_grads",
    )(*[pltpu.with_memory_space_constraint(v, pltpu.HBM) for v in (texts, frames, frame_mask, cotangent.T)])


def solution(mesh):
    return jax.shard_map(
        per_device,
        mesh=mesh,
        in_specs=(P(("blk", "rep"), None), P("blk", None, None), P("blk", None), P(None, "blk")),
        out_specs=(P(("blk", "rep"), None), P(("blk", "rep"), None, None)),
        check_vma=False,
    )
```

```python
import math

import jax
import jax.numpy as jnp
from jax import lax
from jax.experimental import pallas as pl
from jax.experimental.pallas import tpu as pltpu
from jax.sharding import PartitionSpec as P

MESH = pl.DeviceIdType.MESH
EPSILON = 1e-05
FAR_Z = (4, 3, 5, 2, 6, 1, 7, 0)
FAR_X = (2, 1, 3)
NX, NZ, NY = 4, 8, 8
D, FR, C_DEV, ROWS = 512, 48, 16, 4
CHUNK = 128
GROUP = 192
VMEM_LIMIT = 48 * 1024 * 1024
FACTOR = 1.0 / math.sqrt(D)
F32, BF16 = jnp.float32, jnp.bfloat16


def dot(a, b, ca, cb):
    return lax.dot_general(a, b, (((ca,), (cb,)), ((), ())), preferred_element_type=F32)


def swap(v):
    return pltpu.roll(v, 4, axis=1)


def tiles_to_rows(tiles):
    n = tiles.shape[0]
    pairs = tiles.reshape(n // 2, 2, 16, 128)
    low = lax.broadcasted_iota(jnp.int32, (n // 2, 8, 128), 1) < 4
    out = []
    for half in range(2):
        a = pairs[:, 0, 8 * half : 8 * half + 8]
        b = pairs[:, 1, 8 * half : 8 * half + 8]
        out.append(jnp.where(low, a, swap(b)).reshape(4 * n, 128))
        out.append(jnp.where(low, swap(a), b).reshape(4 * n, 128))
    return out


def rows_to_tiles(rows):
    n = rows.shape[0] // 4
    low = lax.broadcasted_iota(jnp.int32, (n // 2, 8, 128), 1) < 4
    blocks = [rows[:, 128 * k : 128 * k + 128].reshape(n // 2, 8, 128) for k in range(4)]
    first, second = [], []
    for half in range(2):
        a, b = blocks[2 * half], blocks[2 * half + 1]
        first.append(jnp.where(low, a, swap(b)))
        second.append(jnp.where(low, swap(a), b))
    first = jnp.concatenate(first, axis=1)
    second = jnp.concatenate(second, axis=1)
    return jnp.stack([first, second], axis=1).reshape(n, 16, 128)


def kernel(
    texts_hbm, frames_ref, mask_hbm, cot_ref, text_out, frame_out,
    texts_ref, mask_ref, frames, cot, tile, texts_in, texts, cot_sel, counts, gram_hi, gram_lo,
    probs_low, weights, scaled, x_send, x_recv, home_send, home_recv,
    core_send, core_recv, frame_send, frame_recv,
    load_sem, swap_send, swap_recv, ag_send, ag_recv, ag_x_send, ag_x_recv,
    rs_x_send, rs_x_recv, rs_send, rs_recv, fr_c_send, fr_c_recv, fr_send, fr_recv,
):
    blk, rep = lax.axis_index("blk"), lax.axis_index("rep")
    core = blk % 2
    high = blk // 2 % 2
    y = high * 4 + rep
    z = blk // 4 % NZ
    x = blk // 32
    clips = rep // 2 * 8
    place = rep % 2
    sign = 1 - 2 * place
    handlers = (y, (y + NY + 2 * sign) % NY, (y + NY - sign) % NY, (y + NY - 3 * sign) % NY)
    peers = (y, *((y + NY + k * sign) % NY for k in (-3, -2, 2, -1)))
    first = (y + 5 * (1 - place)) % NY

    def source(m):
        return (first + (m + 8 - first) % 4) % NY

    def device(xx, zz, yy, cc):
        return (((xx * NZ + zz) * 2 + yy // 4) * 2 + cc, yy % 4)

    sibling = device(x, z, y, 1 - core)
    partner = (blk, rep + 1 - 2 * place)

    def send(src, dst, send_sem, recv_sem, to):
        return pltpu.make_async_remote_copy(
            src_ref=src, dst_ref=dst, send_sem=send_sem, recv_sem=recv_sem, device_id=to, device_id_type=MESH
        )

    started = []

    def start(copy, when=None):
        started.append((copy, when))
        if when is None:
            copy.start()
        else:
            pl.when(when)(copy.start)

    def drain():
        for copy, when in started:
            if when is None:
                copy.wait_send()
            else:
                pl.when(when)(copy.wait_send)

    def arrived(ref, sem):
        pltpu.make_async_copy(ref, ref, sem).wait()

    loads = [pltpu.make_async_copy(cot_ref.at[pl.ds(clips, 8)], cot.at[pl.ds(0, 8)], load_sem.at[2])]
    for g in range(2):
        loads.append(
            pltpu.make_async_copy(
                frames_ref.at[pl.ds(clips + 4 * g, 4)], frames.at[pl.ds(4 * g, 4)], load_sem.at[g]
            )
        )
    barrier = pltpu.get_barrier_semaphore()

    def greet(to):
        pl.semaphore_signal(barrier, inc=1, device_id=to, device_id_type=MESH)

    for dz in FAR_Z:
        for yy in peers[dz == 0 :]:
            greet(device(x, (z + dz) % NZ, yy, core))
    for dx in FAR_X:
        greet(device((x + dx) % NX, z, y, core))
    greet(sibling)
    greet(partner)

    early = (
        pltpu.make_async_copy(texts_hbm, texts_ref, load_sem.at[3]),
        pltpu.make_async_copy(mask_hbm, mask_ref, load_sem.at[4]),
    )
    for load in (*early, *loads):
        load.start()
    for load in early:
        load.wait()
    totals = jnp.sum(mask_ref[pl.ds(clips, 8), :].astype(F32), axis=1, keepdims=True)
    counts[0] = jnp.broadcast_to(totals, (8, CHUNK))

    rows = texts_ref[...].astype(F32)
    tile[...] = jnp.concatenate([rows[:, 128 * k : 128 * k + 128] for k in range(4)], axis=0).astype(BF16)

    pl.semaphore_wait(barrier, 8 * 5 - 1 + 3 + 1 + 1)

    mine = texts_in.at[z, x, rep]
    for dz in FAR_Z:
        for k, yy in enumerate(handlers):
            if dz > 0 or k > 0:
                to = device(x, (z + dz) % NZ, yy, core)
                start(send(tile, mine, ag_send.at[dz, k], ag_recv.at[z], to))
    pltpu.make_async_copy(tile, mine, ag_recv.at[z]).start()

    for load in loads:
        load.wait()
    swaps = (
        (frames.at[pl.ds(0, 8)], frames.at[pl.ds(8, 8)]),
        (cot.at[pl.ds(0, 8)], cot.at[pl.ds(8, 8)]),
        (counts.at[0], counts.at[1]),
    )
    for k, (src, dst) in enumerate(swaps):
        start(send(src, dst, swap_send.at[k], swap_recv.at[k], sibling))

    picked = lax.broadcasted_iota(jnp.int32, (512, CHUNK), 0)
    lane = lax.broadcasted_iota(jnp.int32, (512, CHUNK), 1)
    upper_half = (first + (lane // 4 % 4 + 8 - first) % 4) % NY // 4
    wanted = lane // 16 % 4 * 128 + lane // 64 * 64 + upper_half * 32 + core * 16 + lane % 16
    choose = jnp.where(picked == wanted, 1.0, 0.0).astype(BF16)
    for k, (src, dst) in enumerate(swaps):
        arrived(dst, swap_recv.at[k])
    for k in range(4):
        wide = jnp.concatenate([cot[:, 512 * i + 128 * k : 512 * i + 128 * k + 128] for i in range(NX)], axis=1)
        upper = wide.astype(BF16)
        lower = (wide - upper.astype(F32)).astype(BF16)
        both = dot(jnp.concatenate([upper, lower], axis=0), choose, 1, 0)
        cot_sel[k] = both[:16] + both[16:]
    same = (
        lax.broadcasted_iota(jnp.int32, (GROUP, GROUP), 0) // FR
        == lax.broadcasted_iota(jnp.int32, (GROUP, GROUP), 1) // FR
    )

    def group_frames(g):
        return frames[pl.ds(4 * g, 4)].reshape(GROUP, D)

    for g in range(4):
        block = group_frames(g)
        gram = jnp.where(same, dot(block, block, 1, 1), 0.0)
        upper = gram.astype(BF16)
        gram_hi[g] = upper
        gram_lo[g] = (gram - upper.astype(F32)).astype(BF16)

    def spread(k):
        for zz in (2 * k, 2 * k + 1):
            arrived(texts_in.at[zz, x], ag_recv.at[zz])
        line = texts_in.at[pl.ds(2 * k, 2), x]
        for dx in FAR_X:
            start(send(line, line, ag_x_send.at[k, dx], ag_x_recv.at[k, x], device((x + dx) % NX, z, y, core)))

    def work(k):
        for dx in FAR_X:
            xx = (x + dx) % NX
            arrived(texts_in.at[pl.ds(2 * k, 2), xx], ag_x_recv.at[k, xx])
        columns = slice(CHUNK * k, CHUNK * k + CHUNK)
        tiles = texts_in[2 * k : 2 * k + 2].reshape(32, 16, 128).astype(F32)
        for i, block in enumerate(tiles_to_rows(tiles)):
            texts[columns, 128 * i : 128 * i + 128] = block.astype(BF16)
        chunk = texts[columns, :]
        frame_index = lax.broadcasted_iota(jnp.int32, (FR, CHUNK), 0).astype(F32)
        for g in range(4):
            scores = dot(group_frames(g), chunk, 1, 1)
            kept = []
            for q in range(4):
                c = 4 * g + q
                raw = scores[FR * q : FR * q + FR]
                live = frame_index < counts[c // 8, c % 8 : c % 8 + 1, :]
                masked = jnp.where(live, raw * FACTOR, -1e30)
                top = jnp.max(masked, axis=0, keepdims=True)
                grown = jnp.exp(masked - top)
                probs = grown * (1.0 / jnp.sum(grown, axis=0, keepdims=True))
                low = probs.astype(BF16)
                kept.append((raw, probs, low))
            group_low = jnp.concatenate([low for _, _, low in kept], axis=0)
            probs_low[g, :, columns] = group_low
            against = dot(gram_hi[g], group_low, 1, 0) + dot(gram_lo[g], group_low, 1, 0)
            for q in range(4):
                c = 4 * g + q
                raw, probs, low = kept[q]
                low = low.astype(F32)
                with_pooled = against[FR * q : FR * q + FR]
                square = jnp.maximum(jnp.sum(low * with_pooled, axis=0, keepdims=True), 0.0)
                inner_product = jnp.sum(low * raw, axis=0, keepdims=True)
                inverse = lax.rsqrt(square * (1.0 / D) + EPSILON)
                up = inverse * cot_sel[k, c : c + 1, :] * FACTOR
                back = up * inverse * inverse * inner_product * (1.0 / D)
                prob_grad = up * raw - back * with_pooled
                centred = jnp.sum(probs * prob_grad, axis=0, keepdims=True)
                score_grad = probs * (prob_grad - centred)
                at = slice(FR * q, FR * q + FR)
                weights[g, at, columns] = (up * low + FACTOR * score_grad).astype(BF16)
                scaled[g, at, columns] = (back * low).astype(BF16)
        part = dot(weights[:, :, columns].reshape(16 * FR, CHUNK), frames[...].reshape(16 * FR, D), 0, 0)
        blocks = rows_to_tiles(part).astype(BF16).reshape(2, NX, 4, 16, 128)
        for zz in range(2):
            x_send[k, :, zz] = blocks[zz]
        for dx in FAR_X:
            xx = (x + dx) % NX
            start(
                send(
                    x_send.at[k, xx], x_recv.at[k, dx - 1], rs_x_send.at[k, dx - 1], rs_x_recv.at[k, dx - 1],
                    device(xx, z, y, core),
                )
            )

    def deliver(k):
        total = x_send[k, x].astype(F32)
        for dx in FAR_X:
            arrived(x_recv.at[k, dx - 1], rs_x_recv.at[k, dx - 1])
            total = total + x_recv[k, dx - 1].astype(F32)
        home_send[k] = total.astype(BF16)
        landing = home_recv.at[z, rep]
        for zz in range(2):
            for m in range(4):
                block = home_send.at[k, zz, m]
                stays = jnp.logical_and(rep == m, z == 2 * k + zz)
                copy = send(block, landing, rs_send.at[k, zz, m], rs_recv, device(x, 2 * k + zz, source(m), core))

                @pl.when(stays)
                def _():
                    pltpu.make_async_copy(block, landing, rs_recv).start()

                start(copy, jnp.logical_not(stays))

    def frame_grad(g):
        mixed = jnp.where(same, dot(scaled[g], probs_low[g], 1, 1), 0.0)
        return dot(weights[g], texts[...], 1, 0) - dot(mixed.astype(BF16), group_frames(g), 1, 0)

    def to_sibling(k, g):
        core_send[k] = frame_grad(2 + g).astype(BF16)
        start(send(core_send.at[k], core_recv.at[k], fr_c_send.at[k], fr_c_recv.at[k], sibling))

    def from_sibling(k, g):
        grad = frame_grad(g)
        arrived(core_recv.at[k], fr_c_recv.at[k])
        return grad + core_recv[k].astype(F32)

    for k in range(4):
        spread(k)
    work(0)
    work(1)
    work(2)
    work(3)
    to_sibling(0, 1 - place)
    deliver(0)
    deliver(1)
    frame_send[...] = from_sibling(0, 1 - place).astype(BF16)
    deliver(2)
    start(send(frame_send, frame_recv, fr_send, fr_recv, partner))
    to_sibling(1, place)
    total = from_sibling(1, place)
    deliver(3)

    drain()
    arrived(frame_recv, fr_recv)
    frame_out[...] = (total + frame_recv[...].astype(F32)).astype(BF16).reshape(4, FR, D)

    arrived(home_recv, rs_recv)
    summed = jnp.sum(home_recv[...].reshape(32, 16, 128).astype(F32), axis=0)
    text_out[...] = jnp.concatenate([summed[4 * k : 4 * k + 4] for k in range(4)], axis=1).astype(BF16)


def per_device(texts, frames, frame_mask, cotangent):
    vmem, dma = pltpu.VMEM, pltpu.SemaphoreType.DMA
    whole = pl.BlockSpec(memory_space=pltpu.VMEM)
    remote = pl.BlockSpec(memory_space=pl.ANY)
    return pl.pallas_call(
        kernel,
        out_shape=(
            jax.ShapeDtypeStruct((ROWS, D), BF16),
            jax.ShapeDtypeStruct((4, FR, D), BF16),
        ),
        in_specs=[remote] * 4,
        out_specs=(whole, whole),
        scratch_shapes=[
            vmem((ROWS, D), BF16),
            vmem((C_DEV, FR), jnp.int32),
            vmem((16, FR, D), BF16),
            vmem((16, 2048), F32),
            vmem((16, 128), BF16),
            vmem((NZ, NX, 4, 16, 128), BF16),
            vmem((4 * CHUNK, D), BF16),
            vmem((4, 16, CHUNK), F32),
            vmem((2, 8, CHUNK), F32),
            vmem((4, GROUP, GROUP), BF16),
            vmem((4, GROUP, GROUP), BF16),
            vmem((4, GROUP, 4 * CHUNK), BF16),
            vmem((4, GROUP, 4 * CHUNK), BF16),
            vmem((4, GROUP, 4 * CHUNK), BF16),
            vmem((4, NX, 2, 4, 16, 128), BF16),
            vmem((4, 3, 2, 4, 16, 128), BF16),
            vmem((4, 2, 4, 16, 128), BF16),
            vmem((NZ, 4, 16, 128), BF16),
            vmem((2, GROUP, D), BF16),
            vmem((2, GROUP, D), BF16),
            vmem((GROUP, D), BF16),
            vmem((GROUP, D), BF16),
            dma((5,)), dma((3,)), dma((3,)), dma((NZ, 4)), dma((NZ,)), dma((4, NX)), dma((4, NX)),
            dma((4, 3)), dma((4, 3)), dma((4, 2, 4)), dma, dma((2,)), dma((2,)), dma, dma,
        ],
        compiler_params=pltpu.CompilerParams(
            collective_id=1, has_side_effects=True, vmem_limit_bytes=VMEM_LIMIT
        ),
        name="pooling_grads",
    )(*[pltpu.with_memory_space_constraint(v, pltpu.HBM) for v in (texts, frames, frame_mask, cotangent.T)])


def solution(mesh):
    return jax.shard_map(
        per_device,
        mesh=mesh,
        in_specs=(P(("blk", "rep"), None), P("blk", None, None), P("blk", None), P(None, "blk")),
        out_specs=(P(("blk", "rep"), None), P(("blk", "rep"), None, None)),
        check_vma=False,
    )
```

```python
import math

import jax
import jax.numpy as jnp
from jax import lax
from jax.experimental import pallas as pl
from jax.experimental.pallas import tpu as pltpu
from jax.sharding import PartitionSpec as P

MESH = pl.DeviceIdType.MESH
EPSILON = 1e-05
FAR_Z = (4, 3, 5, 2, 6, 1, 7, 0)
FAR_X = (2, 1, 3)
NX, NZ, NY = 4, 8, 8
D, FR, C_DEV, ROWS = 512, 48, 16, 4
CHUNK = 128
GROUP = 192
VMEM_LIMIT = 48 * 1024 * 1024
FACTOR = 1.0 / math.sqrt(D)
F32, BF16 = jnp.float32, jnp.bfloat16


def dot(a, b, ca, cb):
    return lax.dot_general(a, b, (((ca,), (cb,)), ((), ())), preferred_element_type=F32)


def swap(v):
    return pltpu.roll(v, 4, axis=1)


def tiles_to_rows(tiles):
    n = tiles.shape[0]
    pairs = tiles.reshape(n // 2, 2, 16, 128)
    low = lax.broadcasted_iota(jnp.int32, (n // 2, 8, 128), 1) < 4
    out = []
    for half in range(2):
        a = pairs[:, 0, 8 * half : 8 * half + 8]
        b = pairs[:, 1, 8 * half : 8 * half + 8]
        out.append(jnp.where(low, a, swap(b)).reshape(4 * n, 128))
        out.append(jnp.where(low, swap(a), b).reshape(4 * n, 128))
    return out


def rows_to_tiles(rows):
    n = rows.shape[0] // 4
    low = lax.broadcasted_iota(jnp.int32, (n // 2, 8, 128), 1) < 4
    blocks = [rows[:, 128 * k : 128 * k + 128].reshape(n // 2, 8, 128) for k in range(4)]
    first, second = [], []
    for half in range(2):
        a, b = blocks[2 * half], blocks[2 * half + 1]
        first.append(jnp.where(low, a, swap(b)))
        second.append(jnp.where(low, swap(a), b))
    first = jnp.concatenate(first, axis=1)
    second = jnp.concatenate(second, axis=1)
    return jnp.stack([first, second], axis=1).reshape(n, 16, 128)


def kernel(
    texts_hbm, frames_ref, mask_hbm, cot_ref, text_out, frame_out,
    texts_ref, mask_ref, frames, cot, tile, texts_in, texts, cot_sel, counts, gram_hi, gram_lo,
    probs_low, weights, scaled, x_send, x_recv, home_send, home_recv,
    core_send, core_recv, frame_send, frame_recv,
    load_sem, swap_send, swap_recv, ag_send, ag_recv, ag_x_send, ag_x_recv,
    rs_x_send, rs_x_recv, rs_send, rs_recv, fr_c_send, fr_c_recv, fr_send, fr_recv,
):
    blk, rep = lax.axis_index("blk"), lax.axis_index("rep")
    core = blk % 2
    high = blk // 2 % 2
    y = high * 4 + rep
    z = blk // 4 % NZ
    x = blk // 32
    clips = rep // 2 * 8
    place = rep % 2
    sign = 1 - 2 * place
    handlers = (y, (y + NY + 2 * sign) % NY, (y + NY - sign) % NY, (y + NY - 3 * sign) % NY)
    peers = (y, *((y + NY + k * sign) % NY for k in (-3, -2, 2, -1)))
    first = (y + 5 * (1 - place)) % NY

    def source(m):
        return (first + (m + 8 - first) % 4) % NY

    def device(xx, zz, yy, cc):
        return (((xx * NZ + zz) * 2 + yy // 4) * 2 + cc, yy % 4)

    sibling = device(x, z, y, 1 - core)
    partner = (blk, rep + 1 - 2 * place)

    def send(src, dst, send_sem, recv_sem, to):
        return pltpu.make_async_remote_copy(
            src_ref=src, dst_ref=dst, send_sem=send_sem, recv_sem=recv_sem, device_id=to, device_id_type=MESH
        )

    started = []

    def start(copy, when=None):
        started.append((copy, when))
        if when is None:
            copy.start()
        else:
            pl.when(when)(copy.start)

    def drain():
        for copy, when in started:
            if when is None:
                copy.wait_send()
            else:
                pl.when(when)(copy.wait_send)

    def arrived(ref, sem):
        pltpu.make_async_copy(ref, ref, sem).wait()

    loads = [pltpu.make_async_copy(cot_ref.at[pl.ds(clips, 8)], cot.at[pl.ds(0, 8)], load_sem.at[2])]
    for g in range(2):
        loads.append(
            pltpu.make_async_copy(
                frames_ref.at[pl.ds(clips + 4 * g, 4)], frames.at[pl.ds(4 * g, 4)], load_sem.at[g]
            )
        )
    barrier = pltpu.get_barrier_semaphore()

    def greet(to):
        pl.semaphore_signal(barrier, inc=1, device_id=to, device_id_type=MESH)

    for dz in FAR_Z:
        for yy in peers[dz == 0 :]:
            greet(device(x, (z + dz) % NZ, yy, core))
    for dx in FAR_X:
        greet(device((x + dx) % NX, z, y, core))
    greet(sibling)
    greet(partner)

    early = (
        pltpu.make_async_copy(texts_hbm, texts_ref, load_sem.at[3]),
        pltpu.make_async_copy(mask_hbm, mask_ref, load_sem.at[4]),
    )
    for load in (*early, *loads):
        load.start()
    for load in early:
        load.wait()
    totals = jnp.sum(mask_ref[pl.ds(clips, 8), :].astype(F32), axis=1, keepdims=True)
    counts[0] = jnp.broadcast_to(totals, (8, CHUNK))

    rows = texts_ref[...].astype(F32)
    tile[...] = jnp.concatenate([rows[:, 128 * k : 128 * k + 128] for k in range(4)], axis=0).astype(BF16)

    pl.semaphore_wait(barrier, 8 * 5 - 1 + 3 + 1 + 1)

    mine = texts_in.at[z, x, rep]
    for zz in range(NZ):
        for k in (3, 1, 2, 0):
            copy = send(tile, mine, ag_send.at[zz, k], ag_recv.at[z], device(x, zz, handlers[k], core))
            start(copy, z != zz if k == 0 else None)
    pltpu.make_async_copy(tile, mine, ag_recv.at[z]).start()

    for load in loads:
        load.wait()
    swaps = (
        (frames.at[pl.ds(0, 8)], frames.at[pl.ds(8, 8)]),
        (cot.at[pl.ds(0, 8)], cot.at[pl.ds(8, 8)]),
        (counts.at[0], counts.at[1]),
    )
    for k, (src, dst) in enumerate(swaps):
        start(send(src, dst, swap_send.at[k], swap_recv.at[k], sibling))

    picked = lax.broadcasted_iota(jnp.int32, (512, CHUNK), 0)
    lane = lax.broadcasted_iota(jnp.int32, (512, CHUNK), 1)
    upper_half = (first + (lane // 4 % 4 + 8 - first) % 4) % NY // 4
    wanted = lane // 16 % 4 * 128 + lane // 64 * 64 + upper_half * 32 + core * 16 + lane % 16
    choose = jnp.where(picked == wanted, 1.0, 0.0).astype(BF16)
    for k, (src, dst) in enumerate(swaps):
        arrived(dst, swap_recv.at[k])
    for k in range(4):
        wide = jnp.concatenate([cot[:, 512 * i + 128 * k : 512 * i + 128 * k + 128] for i in range(NX)], axis=1)
        upper = wide.astype(BF16)
        lower = (wide - upper.astype(F32)).astype(BF16)
        both = dot(jnp.concatenate([upper, lower], axis=0), choose, 1, 0)
        cot_sel[k] = both[:16] + both[16:]
    same = (
        lax.broadcasted_iota(jnp.int32, (GROUP, GROUP), 0) // FR
        == lax.broadcasted_iota(jnp.int32, (GROUP, GROUP), 1) // FR
    )

    def group_frames(g):
        return frames[pl.ds(4 * g, 4)].reshape(GROUP, D)

    for g in range(4):
        block = group_frames(g)
        gram = jnp.where(same, dot(block, block, 1, 1), 0.0)
        upper = gram.astype(BF16)
        gram_hi[g] = upper
        gram_lo[g] = (gram - upper.astype(F32)).astype(BF16)

    def spread(k):
        for zz in (2 * k, 2 * k + 1):
            arrived(texts_in.at[zz, x], ag_recv.at[zz])
            line = texts_in.at[zz, x]
            for dx in FAR_X:
                to = device((x + dx) % NX, z, y, core)
                start(send(line, line, ag_x_send.at[zz, dx], ag_x_recv.at[zz, x], to))

    def work(k):
        for dx in FAR_X:
            xx = (x + dx) % NX
            for zz in (2 * k, 2 * k + 1):
                arrived(texts_in.at[zz, xx], ag_x_recv.at[zz, xx])
        columns = slice(CHUNK * k, CHUNK * k + CHUNK)
        tiles = texts_in[2 * k : 2 * k + 2].reshape(32, 16, 128).astype(F32)
        for i, block in enumerate(tiles_to_rows(tiles)):
            texts[columns, 128 * i : 128 * i + 128] = block.astype(BF16)
        chunk = texts[columns, :]
        frame_index = lax.broadcasted_iota(jnp.int32, (FR, CHUNK), 0).astype(F32)
        for g in range(4):
            scores = dot(group_frames(g), chunk, 1, 1)
            kept = []
            for q in range(4):
                c = 4 * g + q
                raw = scores[FR * q : FR * q + FR]
                live = frame_index < counts[c // 8, c % 8 : c % 8 + 1, :]
                masked = jnp.where(live, raw * FACTOR, -1e30)
                top = jnp.max(masked, axis=0, keepdims=True)
                grown = jnp.exp(masked - top)
                probs = grown * (1.0 / jnp.sum(grown, axis=0, keepdims=True))
                low = probs.astype(BF16)
                kept.append((raw, probs, low))
            group_low = jnp.concatenate([low for _, _, low in kept], axis=0)
            probs_low[g, :, columns] = group_low
            against = dot(gram_hi[g], group_low, 1, 0) + dot(gram_lo[g], group_low, 1, 0)
            for q in range(4):
                c = 4 * g + q
                raw, probs, low = kept[q]
                low = low.astype(F32)
                with_pooled = against[FR * q : FR * q + FR]
                square = jnp.maximum(jnp.sum(low * with_pooled, axis=0, keepdims=True), 0.0)
                inner_product = jnp.sum(low * raw, axis=0, keepdims=True)
                inverse = lax.rsqrt(square * (1.0 / D) + EPSILON)
                up = inverse * cot_sel[k, c : c + 1, :] * FACTOR
                back = up * inverse * inverse * inner_product * (1.0 / D)
                prob_grad = up * raw - back * with_pooled
                centred = jnp.sum(probs * prob_grad, axis=0, keepdims=True)
                score_grad = probs * (prob_grad - centred)
                at = slice(FR * q, FR * q + FR)
                weights[g, at, columns] = (up * low + FACTOR * score_grad).astype(BF16)
                scaled[g, at, columns] = (back * low).astype(BF16)
        part = dot(weights[:, :, columns].reshape(16 * FR, CHUNK), frames[...].reshape(16 * FR, D), 0, 0)
        blocks = rows_to_tiles(part).astype(BF16).reshape(2, NX, 4, 16, 128)
        for zz in range(2):
            x_send[k, :, zz] = blocks[zz]
        for dx in FAR_X:
            xx = (x + dx) % NX
            start(
                send(
                    x_send.at[k, xx], x_recv.at[k, dx - 1], rs_x_send.at[k, dx - 1], rs_x_recv.at[k, dx - 1],
                    device(xx, z, y, core),
                )
            )

    def deliver(k):
        total = x_send[k, x].astype(F32)
        for dx in FAR_X:
            arrived(x_recv.at[k, dx - 1], rs_x_recv.at[k, dx - 1])
            total = total + x_recv[k, dx - 1].astype(F32)
        home_send[k] = total.astype(BF16)
        landing = home_recv.at[z, rep]
        for zz in range(2):
            for m in range(4):
                block = home_send.at[k, zz, m]
                stays = jnp.logical_and(rep == m, z == 2 * k + zz)
                copy = send(block, landing, rs_send.at[k, zz, m], rs_recv, device(x, 2 * k + zz, source(m), core))

                @pl.when(stays)
                def _():
                    pltpu.make_async_copy(block, landing, rs_recv).start()

                start(copy, jnp.logical_not(stays))

    def frame_grad(g):
        mixed = jnp.where(same, dot(scaled[g], probs_low[g], 1, 1), 0.0)
        return dot(weights[g], texts[...], 1, 0) - dot(mixed.astype(BF16), group_frames(g), 1, 0)

    def to_sibling(k, g):
        core_send[k] = frame_grad(2 + g).astype(BF16)
        start(send(core_send.at[k], core_recv.at[k], fr_c_send.at[k], fr_c_recv.at[k], sibling))

    def from_sibling(k, g):
        grad = frame_grad(g)
        arrived(core_recv.at[k], fr_c_recv.at[k])
        return grad + core_recv[k].astype(F32)

    for k in range(4):
        spread(k)
    work(0)
    work(1)
    work(2)
    work(3)
    to_sibling(0, 1 - place)
    deliver(0)
    deliver(1)
    frame_send[...] = from_sibling(0, 1 - place).astype(BF16)
    deliver(2)
    start(send(frame_send, frame_recv, fr_send, fr_recv, partner))
    to_sibling(1, place)
    total = from_sibling(1, place)
    deliver(3)

    drain()
    arrived(frame_recv, fr_recv)
    frame_out[...] = (total + frame_recv[...].astype(F32)).astype(BF16).reshape(4, FR, D)

    arrived(home_recv, rs_recv)
    summed = jnp.sum(home_recv[...].reshape(32, 16, 128).astype(F32), axis=0)
    text_out[...] = jnp.concatenate([summed[4 * k : 4 * k + 4] for k in range(4)], axis=1).astype(BF16)


def per_device(texts, frames, frame_mask, cotangent):
    vmem, dma = pltpu.VMEM, pltpu.SemaphoreType.DMA
    whole = pl.BlockSpec(memory_space=pltpu.VMEM)
    remote = pl.BlockSpec(memory_space=pl.ANY)
    return pl.pallas_call(
        kernel,
        out_shape=(
            jax.ShapeDtypeStruct((ROWS, D), BF16),
            jax.ShapeDtypeStruct((4, FR, D), BF16),
        ),
        in_specs=[remote] * 4,
        out_specs=(whole, whole),
        scratch_shapes=[
            vmem((ROWS, D), BF16),
            vmem((C_DEV, FR), jnp.int32),
            vmem((16, FR, D), BF16),
            vmem((16, 2048), F32),
            vmem((16, 128), BF16),
            vmem((NZ, NX, 4, 16, 128), BF16),
            vmem((4 * CHUNK, D), BF16),
            vmem((4, 16, CHUNK), F32),
            vmem((2, 8, CHUNK), F32),
            vmem((4, GROUP, GROUP), BF16),
            vmem((4, GROUP, GROUP), BF16),
            vmem((4, GROUP, 4 * CHUNK), BF16),
            vmem((4, GROUP, 4 * CHUNK), BF16),
            vmem((4, GROUP, 4 * CHUNK), BF16),
            vmem((4, NX, 2, 4, 16, 128), BF16),
            vmem((4, 3, 2, 4, 16, 128), BF16),
            vmem((4, 2, 4, 16, 128), BF16),
            vmem((NZ, 4, 16, 128), BF16),
            vmem((2, GROUP, D), BF16),
            vmem((2, GROUP, D), BF16),
            vmem((GROUP, D), BF16),
            vmem((GROUP, D), BF16),
            dma((5,)), dma((3,)), dma((3,)), dma((NZ, 4)), dma((NZ,)), dma((NZ, NX)), dma((NZ, NX)),
            dma((4, 3)), dma((4, 3)), dma((4, 2, 4)), dma, dma((2,)), dma((2,)), dma, dma,
        ],
        compiler_params=pltpu.CompilerParams(
            collective_id=1, has_side_effects=True, vmem_limit_bytes=VMEM_LIMIT
        ),
        name="pooling_grads",
    )(*[pltpu.with_memory_space_constraint(v, pltpu.HBM) for v in (texts, frames, frame_mask, cotangent.T)])


def solution(mesh):
    return jax.shard_map(
        per_device,
        mesh=mesh,
        in_specs=(P(("blk", "rep"), None), P("blk", None, None), P("blk", None), P(None, "blk")),
        out_specs=(P(("blk", "rep"), None), P(("blk", "rep"), None, None)),
        check_vma=False,
    )
```
